512 devices in a mesh: gz: 8 (over x, core), xy: 64 (over y, z).
Axes of the slice: x: 4, y: 8, z: 8, core: 2. Of those that a mesh axis runs over, the one named last changes fastest.
Arguments:
- tile_planes: float32 [8, 6144, 2048], P('gz', 'xy'), may hold values from 0.5 to 2
- plane_owner: int32 [8, 6144, 1], P('gz', 'xy'), may hold values from 0 to 63, as said below
- plane_slot: int32 [8, 6144], P('gz', 'xy'), may hold values from 0 to 95, as said below
- view_shift: int32 [6], replicated, may hold values from -16 to 16
- psf_z: float32 [6, 33], replicated, may hold values from 0.05 to 1
- psf_x: float32 [6, 33], replicated, may hold values from 0.05 to 1
- psf_y: float32 [6, 33], replicated, may hold values from 0.05 to 1
- background: float32 [6], replicated, may hold values from 0.1 to 0.5
- initial_estimate: float32 [128, 1024, 128], P('gz', 'xy'), may hold values from 0.5 to 2
Outputs:
- deconvolved: float32 [128, 1024, 128], P('gz', 'xy')
The draws below stay inside these ranges and needn't reach their ends.
Inputs may be any that keep to these rules, and one draw needn't show every extreme that they name: `plane_owner`: among the 96 rows of one device no brick owner is named more than 3 times, and some owner exactly 3 times. Within one z-slab every brick owner is named by exactly 96 rows. `plane_slot`: within one z-slab, the rows that name one brick owner carry each slot of 0 to 95 exactly once.
All inputs are finite; a program needn't handle non-finite values.
Results may differ from the reference program's by a relative error of at most 0.0001.
Values sent between devices are 32-bit elements; how exact they have to be, the bound alone decides.
No kernel may reach another device: no remote copies, remote signals or barrier semaphores. Data moves between devices by JAX's collectives and lax.ppermute only.
A program may use at most 64 MiB of HBM per device.

```python
import math
import jax
import jax.numpy as jnp
from jax import lax

V = 6
R = 16
TAPS = 33
BZ = 16
BX = 16
NY = 128
SEND = 3
SRC = 96
ITERS = 2
NZ = 128
NX = 1024
N_GZ = 8
N_XY = 64


def route_tables(key):
    size = V * BZ
    span = N_XY
    keys = jax.random.split(key, 5)
    full = size // SEND
    offsets = jnp.arange(span, dtype=jnp.int32)
    profile = jnp.where(offsets < full, SEND, jnp.where(offsets == full, size - full * SEND, 0)).astype(jnp.int32)
    perm_n = jax.vmap(lambda k: jax.random.permutation(k, span).astype(jnp.int32))
    picks = perm_n(jax.random.split(keys[0], N_GZ))
    pattern = profile[picks]
    src_perm = perm_n(jax.random.split(keys[1], N_GZ))
    dst_perm = perm_n(jax.random.split(keys[2], N_GZ))
    diff = (dst_perm[:, None, :] - src_perm[:, :, None]) % span
    counts = jax.vmap(lambda p, d: p[d])(pattern, diff)
    ends = jnp.cumsum(counts, axis=2)
    starts_row = ends - counts
    position = jnp.arange(size, dtype=jnp.int32)
    owner_rows = jnp.sum((ends[:, :, None, :] <= position[None, None, :, None]).astype(jnp.int32), axis=3)
    start_pick = jnp.take_along_axis(starts_row, owner_rows, axis=2)
    rank = position[None, None, :] - start_pick
    starts_src = jnp.cumsum(counts, axis=1) - counts
    base = jnp.take_along_axis(starts_src, owner_rows, axis=2)
    index = base + rank
    perm_s = jax.vmap(lambda k: jax.random.permutation(k, size).astype(jnp.int32))
    sigma = perm_s(jax.random.split(keys[3], N_GZ * span)).reshape(N_GZ, span, size)
    slabs = jnp.arange(N_GZ, dtype=jnp.int32)[:, None, None]
    slots = sigma[slabs, owner_rows, index]
    shuffle = perm_s(jax.random.split(keys[4], N_GZ * span)).reshape(N_GZ, span, size)
    owner_rows = jnp.take_along_axis(owner_rows, shuffle, axis=2)
    slots = jnp.take_along_axis(slots, shuffle, axis=2)
    return (owner_rows.reshape(N_GZ, span * size), slots.reshape(N_GZ, span * size))


def draw_plane_owner(key, part):
    owners, slots = route_tables(key)
    return owners.reshape(N_GZ, N_XY * SRC, 1).astype(jnp.int32)


def draw_plane_slot(key, part):
    owners, slots = route_tables(key)
    return slots.astype(jnp.int32)


def touch_ends(entries, key, least, largest):
    longest = entries.shape.index(max(entries.shape))
    spots = []
    for shift in (0, 1):
        where = [jax.random.randint(jax.random.fold_in(key, axis), (), 0, length) for axis, length in enumerate(entries.shape)]
        where[longest] = (where[longest] + shift) % entries.shape[longest]
        spots.append(tuple(where))
    return entries.at[spots[0]].set(least).at[spots[1]].set(largest)


def block_scale(rng, extent, shards, smallest, top_value):
    def one(dim, shards_of):
        draws = jax.random.uniform(jax.random.fold_in(jax.random.fold_in(rng, 6), dim), (shards_of,), jnp.float32, smallest / len(shards), top_value / len(shards))
        return jnp.repeat(jnp.exp(draws), extent[dim] // shards_of).reshape((-1,) + (1,) * (len(extent) - dim - 1))

    level = one(*shards[0])
    for cut in shards[1:]:
        level = level * one(*cut)
    return level


def setup_inputs(seed: int = 0) -> dict:
    key_list = jax.random.split(jax.random.key(seed), 10)
    return {
        "tile_planes": jnp.clip(jnp.exp(math.log(2.0) - 1.3862944 * jax.random.uniform(key_list[0], (N_GZ, N_XY * SRC, BX * NY), jnp.float32) ** block_scale(key_list[0], (N_GZ, N_XY * SRC, BX * NY), ((0, 8), (1, 64)), -0.2, 0.2)), 0.5, 2.0),
        "plane_owner": draw_plane_owner(jax.random.fold_in(key_list[9], 71), 0),
        "plane_slot": draw_plane_slot(jax.random.fold_in(key_list[9], 71), 0),
        "view_shift": touch_ends(jax.random.randint(key_list[3], (V,), 0 - R, R + 1), jax.random.fold_in(key_list[3], 1), 0 - R, R).astype(jnp.int32),
        "psf_z": jnp.clip(jnp.exp(jax.random.uniform(key_list[4], (V, TAPS), jnp.float32, math.log(0.05), math.log(1.0))), 0.05, 1.0),
        "psf_x": jnp.clip(jnp.exp(jax.random.uniform(key_list[5], (V, TAPS), jnp.float32, math.log(0.05), math.log(1.0))), 0.05, 1.0),
        "psf_y": jnp.clip(jnp.exp(jax.random.uniform(key_list[6], (V, TAPS), jnp.float32, math.log(0.05), math.log(1.0))), 0.05, 1.0),
        "background": jnp.clip(jnp.exp(jax.random.uniform(key_list[7], (V,), jnp.float32, math.log(0.1), math.log(0.5))), 0.1, 0.5),
        "initial_estimate": jnp.clip(jnp.exp(math.log(2.0) - 1.3862944 * jax.random.uniform(key_list[8], (NZ, NX, NY), jnp.float32) ** block_scale(key_list[8], (NZ, NX, NY), ((0, 8), (1, 64)), -0.2, 0.2)), 0.5, 2.0),
    }


def along(field, taps, axis):
    shape = [1, 1, 1]
    shape[axis] = taps.shape[0]
    kernel = taps.reshape([1, 1] + shape)
    pads = [(0, 0), (0, 0), (0, 0)]
    pads[axis] = (R, R)
    result = lax.conv_general_dilated(field[None, None], kernel, (1, 1, 1), pads,
                                      precision=lax.Precision.HIGHEST)
    return result[0, 0]


def shifted_y(field, taps, offset):
    padded = jnp.pad(field, ((0, 0), (0, 0), (2 * R, 2 * R)))
    kernel = taps.reshape(1, 1, 1, 1, taps.shape[0])
    valid = lax.conv_general_dilated(padded[None, None], kernel, (1, 1, 1), [(0, 0), (0, 0), (0, 0)],
                                     precision=lax.Precision.HIGHEST)[0, 0]
    start = (R - offset).astype(jnp.int32)
    return lax.dynamic_slice_in_dim(valid, start, field.shape[2], 2)


def reference(tile_planes, plane_owner, plane_slot, view_shift, psf_z, psf_x, psf_y, background, initial_estimate):
    owner = plane_owner[..., 0]
    slabs = jnp.broadcast_to(jnp.arange(N_GZ, dtype=jnp.int32)[:, None], owner.shape)
    view_of = plane_slot // BZ
    depth_of = slabs * BZ + plane_slot % BZ
    rows = tile_planes.reshape(N_GZ, N_XY * SRC, BX, NY)
    data = jnp.zeros((V, NZ, N_XY, BX, NY), jnp.float32)
    data = data.at[view_of, depth_of, owner].add(rows).reshape(V, NZ, NX, NY)
    axial_norm_weights = psf_z / jnp.sum(psf_z, axis=1, keepdims=True)
    lateral_norm_weights = psf_x / jnp.sum(psf_x, axis=1, keepdims=True)
    norm_y = psf_y / jnp.sum(psf_y, axis=1, keepdims=True)
    estimate = initial_estimate
    for step in range(ITERS):
        summed_correction = jnp.zeros_like(estimate)
        for view_volume in range(V):
            shift = view_shift[view_volume]
            blur = along(along(estimate, axial_norm_weights[view_volume], 0), lateral_norm_weights[view_volume], 1)
            blur = shifted_y(blur, norm_y[view_volume], shift) + background[view_volume]
            ratio = data[view_volume] / blur
            back = along(along(ratio, axial_norm_weights[view_volume][::-1], 0), lateral_norm_weights[view_volume][::-1], 1)
            back = shifted_y(back, norm_y[view_volume][::-1], -shift)
            summed_correction = summed_correction + back
        estimate = estimate * (summed_correction / V)
    return estimate
```

```python
import jax
import jax.numpy as jnp
from jax import lax
from jax.experimental import pallas as pl
from jax.experimental.pallas import tpu as pltpu
from jax.sharding import PartitionSpec as P

ITERS = 2
VIEWS = 6
TAPS = 33
R = 16
BZ = 16
BX = 16
NY = 128
SEND = 3
SRC = 96
PEERS = 64
EX = BX + 2 * R
EZ = BZ + 2 * R
SLOTS = VIEWS * BZ
CHUNK = SEND * BX + 1
VU = VIEWS * BX
F32 = jnp.float32
BF16 = jnp.bfloat16

VMEM = pl.BlockSpec(memory_space=pltpu.VMEM)
SMEM = pl.BlockSpec(memory_space=pltpu.SMEM)


def params(mib):
    return pltpu.CompilerParams(vmem_limit_bytes=mib * 1024 * 1024)


def shape(dims, dtype=F32):
    return jax.ShapeDtypeStruct(dims, dtype)


def split(value):
    high = value.astype(BF16)
    return high, (value - high.astype(F32)).astype(BF16)


def pack_kernel(owner, slot, planes, send, rows, count, named):
    for group in range(SRC // 8):
        for column in range(BX):
            rows[pl.ds(group * 8 * BX + column, 8, stride=BX), :] = planes[
                group * 8 : group * 8 + 8, column * NY : (column + 1) * NY
            ]

    def clear(peer, carry):
        count[peer] = 0
        for rank in range(SEND):
            named[peer * SEND + rank] = SLOTS
        return carry

    lax.fori_loop(0, PEERS, clear, 0)

    def place(plane, carry):
        peer = owner[plane]
        rank = count[peer]
        count[peer] = rank + 1
        named[peer * SEND + rank] = slot[plane]
        start = peer * CHUNK + rank * BX
        send[pl.ds(start, BX), :] = rows[pl.ds(pl.multiple_of(plane * BX, BX), BX), :]
        return carry

    lax.fori_loop(0, SRC, place, 0)
    lane = lax.broadcasted_iota(jnp.int32, (1, NY), 1)

    def tell(peer, carry):
        row = jnp.full((1, NY), named[peer * SEND], jnp.int32)
        for rank in range(1, SEND):
            row = jnp.where(lane == rank, named[peer * SEND + rank], row)
        send[pl.ds(peer * CHUNK + SEND * BX, 1), :] = row.astype(F32)
        return carry

    lax.fori_loop(0, PEERS, tell, 0)


def pack(owner, slot, planes):
    return pl.pallas_call(
        pack_kernel,
        out_shape=shape((PEERS * CHUNK, NY)),
        in_specs=[SMEM, SMEM, VMEM],
        out_specs=VMEM,
        scratch_shapes=[
            pltpu.VMEM((SRC * BX, NY), F32),
            pltpu.SMEM((PEERS,), jnp.int32),
            pltpu.SMEM((PEERS * SEND,), jnp.int32),
        ],
        compiler_params=params(16),
        name="pack_planes",
    )(owner, slot, planes)


def weight_kernel(taps, shift, x_fwd, x_back, y_fwd, y_back):
    row = lax.broadcasted_iota(jnp.int32, (BX, NY), 0)
    lane = lax.broadcasted_iota(jnp.int32, (BX, NY), 1)
    bands = []
    for view in range(VIEWS):
        band = jnp.zeros((BX, NY), F32)
        for tap in range(TAPS):
            band = jnp.where(lane - row == tap, taps[VIEWS + view, tap], band)
        bands.append(band)
    band = jnp.concatenate(bands + [jnp.zeros((NY - VU, NY), F32)], axis=0)
    high, low = split(band[:VU, :EX])
    x_fwd[...] = jnp.concatenate([high, low, high], axis=1)
    high, low = split(jnp.transpose(band)[:EX, :VU])
    x_back[...] = jnp.concatenate([high, low, high], axis=1)
    row = lax.broadcasted_iota(jnp.int32, (NY, NY), 0)
    lane = lax.broadcasted_iota(jnp.int32, (NY, NY), 1)

    def along_y(view, carry):
        offset = lane - row + R + shift[view]
        back = jnp.zeros((NY, NY), F32)
        for tap in range(TAPS):
            back = jnp.where(offset == tap, taps[2 * VIEWS + view, tap], back)
        high, low = split(back)
        y_back[view] = jnp.concatenate([high, low, high], axis=0)
        high, low = split(jnp.transpose(back))
        y_fwd[view] = jnp.concatenate([high, low, high], axis=0)
        return carry

    lax.fori_loop(0, VIEWS, along_y, 0)


def weights(taps, shift):
    return pl.pallas_call(
        weight_kernel,
        out_shape=[
            shape((VU, 3 * EX), BF16),
            shape((EX, 3 * VU), BF16),
            shape((VIEWS, 3 * NY, NY), BF16),
            shape((VIEWS, 3 * NY, NY), BF16),
        ],
        in_specs=[SMEM, SMEM],
        out_specs=[VMEM] * 4,
        compiler_params=params(16),
        name="operator_matrices",
    )(taps, shift)


def dot(left, right):
    return jnp.dot(left, right, preferred_element_type=F32)


def along_x_fwd(x_fwd, pieces, starts, wide):
    matrix = x_fwd[...]
    for piece, start in zip(pieces, starts):

        def one(plane, carry):
            high, low = split(piece[plane])
            wide[start + plane] = dot(matrix, jnp.concatenate([high, high, low], axis=0))
            return carry

        lax.fori_loop(0, BZ, one, 0, unroll=4)


def along_z_fwd(taps, wide, narrow):
    def one(index, carry):
        view = index // 2
        rows = pl.ds(pl.multiple_of(index * 8, 8), 8)
        window = [wide[plane, rows, :] for plane in range(BZ)]
        sums = [None] * BZ
        for tap in range(TAPS):
            if tap:
                window = window[1:] + [wide[tap + BZ - 1, rows, :]]
            weight = jnp.full((8, NY), taps[view, tap], F32)
            for plane in range(BZ):
                term = weight * window[plane]
                sums[plane] = term if tap == 0 else sums[plane] + term
        base = view * BZ * BX + (index % 2) * 8
        for plane in range(BZ):
            narrow[pl.ds(pl.multiple_of(base + plane * BX, 8), 8), :] = sums[plane]
        return carry

    lax.fori_loop(0, 2 * VIEWS, one, 0)


def rows_of(view):
    return pl.ds(pl.multiple_of(view * BZ * BX, BZ * BX), BZ * BX)


def along_y(matrix, value):
    high, low = split(value)
    return dot(jnp.concatenate([high, high, low], axis=1), matrix)


def placed(core):
    inside = jnp.where(core == 0, 2 * R, 0)
    outside = jnp.where(core == 0, 0, 2 * R)
    return [R, inside, outside]


def forward_kernel(core, taps, background, x_fwd, y_fwd, own, inside, outside, blur, wide, narrow):
    along_x_fwd(x_fwd, [own, inside, outside], placed(core[0]), wide)
    along_z_fwd(taps, wide, narrow)

    def one(view, carry):
        blur[rows_of(view), :] = along_y(y_fwd[view], narrow[rows_of(view), :]) + background[view]
        return carry

    lax.fori_loop(0, VIEWS, one, 0)


def forward(core, taps, background, x_fwd, y_fwd, own, inside, outside):
    return pl.pallas_call(
        forward_kernel,
        out_shape=shape((SLOTS * BX, NY)),
        in_specs=[SMEM] * 3 + [VMEM] * 5,
        out_specs=VMEM,
        scratch_shapes=[
            pltpu.VMEM((EZ, VU, NY), F32),
            pltpu.VMEM((SLOTS * BX, NY), F32),
        ],
        compiler_params=params(24),
        name="forward",
    )(core, taps, background, x_fwd, y_fwd, own, inside, outside)


def along_z_back(taps, narrow, wide):
    def one(index, carry):
        view = index // 2
        rows = pl.ds(pl.multiple_of(index * 8, 8), 8)
        base = view * BZ * BX + (index % 2) * 8
        planes = [
            narrow[pl.ds(pl.multiple_of(base + plane * BX, 8), 8), :] for plane in range(BZ)
        ]
        sums = [None] * BZ
        for tap in range(TAPS):
            weight = jnp.full((8, NY), taps[view, tap], F32)
            for plane in range(BZ):
                term = weight * planes[plane]
                sums[plane] = term if sums[plane] is None else sums[plane] + term
            wide[tap, rows, :] = sums[0]
            sums = sums[1:] + [None]
        for plane in range(BZ - 1):
            wide[TAPS + plane, rows, :] = sums[plane]
        return carry

    lax.fori_loop(0, 2 * VIEWS, one, 0)


def along_x_back(x_back, wide, pieces, starts):
    matrix = x_back[...]
    for piece, start in zip(pieces, starts):

        def one(plane, carry):
            high, low = split(wide[start + plane])
            piece[plane] = dot(matrix, jnp.concatenate([high, high, low], axis=0))
            return carry

        lax.fori_loop(0, BZ, one, 0, unroll=4)


def back_steps(core, taps, x_back, y_back, data, blur, own, inside, outside, wide, narrow):
    def one(view, carry):
        ratio = data[rows_of(view), :] / blur[rows_of(view), :]
        narrow[rows_of(view), :] = along_y(y_back[view], ratio)
        return carry

    lax.fori_loop(0, VIEWS, one, 0)
    along_z_back(taps, narrow, wide)
    along_x_back(x_back, wide, [own, inside, outside], placed(core[0]))


def first_back_kernel(
    core, taps, x_back, y_back, got, blur, data, own, inside, outside, wide, narrow, names, slots, sem
):
    names[...] = got[pl.ds(SEND * BX, PEERS, stride=CHUNK), :].astype(jnp.int32)
    copy = pltpu.make_async_copy(names, slots, sem)
    copy.start()
    copy.wait()

    def unpack(peer, carry):
        for rank in range(SEND):
            slot = slots[peer, rank]
            data[pl.ds(pl.multiple_of(slot * BX, BX), BX), :] = got[
                pl.ds(peer * CHUNK + rank * BX, BX), :
            ]
        return carry

    lax.fori_loop(0, PEERS, unpack, 0)
    back_steps(core, taps, x_back, y_back, data, blur, own, inside, outside, wide, narrow)


def first_back(core, taps, x_back, y_back, got, blur):
    return pl.pallas_call(
        first_back_kernel,
        out_shape=[shape(((SLOTS + 1) * BX, NY))] + [shape((BZ, EX, NY))] * 3,
        in_specs=[SMEM] * 2 + [VMEM] * 4,
        out_specs=[VMEM] * 4,
        scratch_shapes=[
            pltpu.VMEM((EZ, VU, NY), F32),
            pltpu.VMEM((SLOTS * BX, NY), F32),
            pltpu.VMEM((PEERS, NY), jnp.int32),
            pltpu.SMEM((PEERS, NY), jnp.int32),
            pltpu.SemaphoreType.DMA,
        ],
        compiler_params=params(24),
        name="first_back",
    )(core, taps, x_back, y_back, got, blur)


def later_kernel(
    core, taps, background, x_fwd, y_fwd, x_back, y_back, e_own, e_inside, e_outside, data,
    own, inside, outside, wide, narrow, blur,
):
    forward_kernel(
        core, taps, background, x_fwd, y_fwd, e_own, e_inside, e_outside, blur, wide, narrow
    )
    back_steps(core, taps, x_back, y_back, data, blur, own, inside, outside, wide, narrow)


def later(core, taps, background, x_fwd, y_fwd, x_back, y_back, e_own, e_inside, e_outside, data):
    return pl.pallas_call(
        later_kernel,
        out_shape=[shape((BZ, EX, NY))] * 3,
        in_specs=[SMEM] * 3 + [VMEM] * 8,
        out_specs=[VMEM] * 3,
        scratch_shapes=[
            pltpu.VMEM((EZ, VU, NY), F32),
            pltpu.VMEM((SLOTS * BX, NY), F32),
            pltpu.VMEM((SLOTS * BX, NY), F32),
        ],
        compiler_params=params(24),
        name="forward_and_back",
    )(core, taps, background, x_fwd, y_fwd, x_back, y_back, e_own, e_inside, e_outside, data)


def swaps(first, count):
    pairs = [(i, i + 1) for i in range(first, count - 1, 2)]
    return pairs + [(j, i) for i, j in pairs]


def gathered(block, odd):
    even_pair = lax.ppermute(block, "xy", swaps(0, PEERS))
    odd_pair = lax.ppermute(block, "xy", swaps(1, PEERS))
    left = jnp.where(odd, even_pair, odd_pair)
    right = jnp.where(odd, odd_pair, even_pair)
    own = jnp.concatenate([left, block, right], axis=1)
    count = lax.axis_size("gz")
    return own, lax.ppermute(own, "gz", swaps(0, count)), lax.ppermute(own, "gz", swaps(1, count))


def scattered(own, inside, outside, odd):
    count = lax.axis_size("gz")
    total = (
        own
        + lax.ppermute(inside, "gz", swaps(0, count))
        + lax.ppermute(outside, "gz", swaps(1, count))
    )
    left, right = total[:, :R], total[:, R + BX :]
    even_pair = lax.ppermute(jnp.where(odd, left, right), "xy", swaps(0, PEERS))
    odd_pair = lax.ppermute(jnp.where(odd, right, left), "xy", swaps(1, PEERS))
    return total[:, R : R + BX] + even_pair + odd_pair


def local(
    tile_planes,
    plane_owner,
    plane_slot,
    view_shift,
    psf_z,
    psf_x,
    psf_y,
    background,
    initial_estimate,
):
    core = lax.rem(lax.axis_index("gz"), 2).astype(jnp.int32).reshape(1)
    odd = lax.rem(lax.axis_index("xy"), 2) == 1
    send = pack(plane_owner.reshape(SRC), plane_slot.reshape(SRC), tile_planes[0])
    got = lax.all_to_all(
        send.reshape(PEERS, 1, CHUNK * NY), "xy", split_axis=0, concat_axis=0, tiled=True
    ).reshape(PEERS * CHUNK, NY)
    psf = jnp.concatenate([psf_z, psf_x, psf_y], axis=0)
    taps = psf / jnp.sum(psf, axis=1, keepdims=True)
    x_fwd, x_back, y_fwd, y_back = weights(taps, view_shift)
    estimate = initial_estimate
    for step in range(ITERS):
        pieces = gathered(estimate, odd)
        if step == 0:
            blur = forward(core, taps, background, x_fwd, y_fwd, *pieces)
            data, *parts = first_back(core, taps, x_back, y_back, got, blur)
        else:
            parts = later(
                core, taps, background, x_fwd, y_fwd, x_back, y_back, *pieces, data
            )
        estimate = estimate * (scattered(*parts, odd) / VIEWS)
    return estimate


def solution(mesh):
    return jax.shard_map(
        local,
        mesh=mesh,
        in_specs=(
            P("gz", "xy", None),
            P("gz", "xy", None),
            P("gz", "xy"),
            P(),
            P(),
            P(),
            P(),
            P(),
            P("gz", "xy", None),
        ),
        out_specs=P("gz", "xy", None),
        check_vma=False,
    )
```

```python
import jax
import jax.numpy as jnp
from jax import lax
from jax.experimental import pallas as pl
from jax.experimental.pallas import tpu as pltpu
from jax.sharding import PartitionSpec as P

ITERS = 2
VIEWS = 6
TAPS = 33
R = 16
BZ = 16
BX = 16
NY = 128
SEND = 3
SRC = 96
PEERS = 64
EX = BX + 2 * R
EZ = BZ + 2 * R
SLOTS = VIEWS * BZ
CHUNK = SEND * BX + 1
VU = VIEWS * BX
PITCH = VU + 8
LINE = BZ + 8
AT_ONCE = 4
F32 = jnp.float32
BF16 = jnp.bfloat16

VMEM = pl.BlockSpec(memory_space=pltpu.VMEM)
SMEM = pl.BlockSpec(memory_space=pltpu.SMEM)


def params(mib):
    return pltpu.CompilerParams(vmem_limit_bytes=mib * 1024 * 1024)


def shape(dims, dtype=F32):
    return jax.ShapeDtypeStruct(dims, dtype)


def split(value):
    high = value.astype(BF16)
    return high, (value - high.astype(F32)).astype(BF16)


def pack_kernel(owner, slot, planes, send, rows, count):
    for peer in range(PEERS):
        count[peer] = 0
    send[pl.ds(SEND * BX, PEERS, stride=CHUNK), :] = jnp.full((PEERS, NY), SLOTS, F32)
    for group in range(SRC // 8):
        for column in range(BX):
            rows[pl.ds(group * 8 * BX + column, 8, stride=BX), :] = planes[
                group * 8 : group * 8 + 8, column * NY : (column + 1) * NY
            ]
    lane = lax.broadcasted_iota(jnp.int32, (1, NY), 1)

    def place(plane, carry):
        peer = owner[plane]
        rank = count[peer]
        count[peer] = rank + 1
        start = peer * CHUNK
        send[pl.ds(start + rank * BX, BX), :] = rows[pl.ds(pl.multiple_of(plane * BX, BX), BX), :]
        pltpu.store(
            send.at[pl.ds(start + SEND * BX, 1), :],
            jnp.full((1, NY), slot[plane], jnp.int32).astype(F32),
            mask=lane == rank,
        )
        return carry

    lax.fori_loop(0, SRC, place, 0, unroll=8)


def pack(owner, slot, planes):
    return pl.pallas_call(
        pack_kernel,
        out_shape=shape((PEERS * CHUNK, NY)),
        in_specs=[SMEM, SMEM, VMEM],
        out_specs=VMEM,
        scratch_shapes=[
            pltpu.VMEM((SRC * BX, NY), F32),
            pltpu.SMEM((PEERS,), jnp.int32),
        ],
        compiler_params=params(16),
        name="pack_planes",
    )(owner, slot, planes)


def bands(taps, first):
    row = lax.broadcasted_iota(jnp.int32, (BX, NY), 0)
    lane = lax.broadcasted_iota(jnp.int32, (BX, NY), 1)
    each = []
    for view in range(VIEWS):
        band = jnp.zeros((BX, NY), F32)
        for tap in range(TAPS):
            band = jnp.where(lane - row == tap, taps[first + view, tap], band)
        each.append(band)
    return jnp.concatenate(each + [jnp.zeros((NY - VU, NY), F32)], axis=0)


def by_terms(value):
    high, low = split(value)
    return jnp.concatenate([high, low, high], axis=1)


def weight_kernel(taps, shift, z_fwd, z_back, x_fwd, x_back, y_fwd, y_back):
    band = bands(taps, 0)
    turned = jnp.transpose(band)[:EZ]
    for view in range(VIEWS):
        z_fwd[view] = by_terms(band[view * BZ : (view + 1) * BZ, :EZ])
        z_back[view] = by_terms(turned[:, view * BZ : (view + 1) * BZ])
    band = bands(taps, VIEWS)
    x_fwd[...] = by_terms(band[:VU, :EX])
    x_back[...] = by_terms(jnp.transpose(band)[:EX, :VU])
    row = lax.broadcasted_iota(jnp.int32, (NY, NY), 0)
    lane = lax.broadcasted_iota(jnp.int32, (NY, NY), 1)

    def along_y(view, carry):
        offset = lane - row + R + shift[view]
        back = jnp.zeros((NY, NY), F32)
        for tap in range(TAPS):
            back = jnp.where(offset == tap, taps[2 * VIEWS + view, tap], back)
        high, low = split(back)
        y_back[view] = jnp.concatenate([high, low, high], axis=0)
        high, low = split(jnp.transpose(back))
        y_fwd[view] = jnp.concatenate([high, low, high], axis=0)
        return carry

    lax.fori_loop(0, VIEWS, along_y, 0)


def weights(taps, shift):
    return pl.pallas_call(
        weight_kernel,
        out_shape=[
            shape((VIEWS, BZ, 3 * EZ), BF16),
            shape((VIEWS, EZ, 3 * BZ), BF16),
            shape((VU, 3 * EX), BF16),
            shape((EX, 3 * VU), BF16),
            shape((VIEWS, 3 * NY, NY), BF16),
            shape((VIEWS, 3 * NY, NY), BF16),
        ],
        in_specs=[SMEM, SMEM],
        out_specs=[VMEM] * 6,
        compiler_params=params(16),
        name="operator_matrices",
    )(taps, shift)


def dot(left, right):
    return jnp.dot(left, right, preferred_element_type=F32)


def terms(value):
    high, low = split(value)
    return jnp.concatenate([high, high, low], axis=0)


def along_x_fwd(matrix, pieces, starts, wide):
    matrix = matrix[...]
    for piece, start in zip(pieces, starts):
        for first in range(0, BZ, AT_ONCE):
            planes = range(first, first + AT_ONCE)
            product = dot(matrix, jnp.concatenate([terms(piece[p]) for p in planes], axis=1))
            for i, plane in enumerate(planes):
                rows = pl.ds(pl.multiple_of((start + plane) * PITCH, 8), VU)
                wide[rows, :] = product[:, i * NY : (i + 1) * NY]


def along_z_fwd(matrix, wide, narrow):
    def one(view, carry):
        for first in range(0, BX, AT_ONCE):
            columns = range(first, first + AT_ONCE)
            loaded = [wide[pl.ds(view * BX + c, EZ, stride=PITCH), :] for c in columns]
            product = dot(matrix[view], jnp.concatenate([terms(v) for v in loaded], axis=1))
            for i, column in enumerate(columns):
                rows = pl.ds(pl.multiple_of((view * BX + column) * BZ, BZ), BZ)
                narrow[rows, :] = product[:, i * NY : (i + 1) * NY]
        return carry

    lax.fori_loop(0, VIEWS, one, 0)


def rows_of(view):
    return pl.ds(view * BZ * BX, BZ * BX)


def along_y(matrix, value):
    high, low = split(value)
    return dot(jnp.concatenate([high, high, low], axis=1), matrix)


def placed(core):
    inside = jnp.where(core == 0, 2 * R, 0)
    outside = jnp.where(core == 0, 0, 2 * R)
    return [R, inside, outside]


def forward_kernel(
    core, background, z_fwd, x_fwd, y_fwd, own, inside, outside, blur, wide, narrow
):
    along_x_fwd(x_fwd, [own, inside, outside], placed(core[0]), wide)
    along_z_fwd(z_fwd, wide, narrow)
    for view in range(VIEWS):
        blur[rows_of(view), :] = along_y(y_fwd[view], narrow[rows_of(view), :]) + background[view]


def forward(core, background, z_fwd, x_fwd, y_fwd, own, inside, outside):
    return pl.pallas_call(
        forward_kernel,
        out_shape=shape((SLOTS * BX, NY)),
        in_specs=[SMEM] * 2 + [VMEM] * 6,
        out_specs=VMEM,
        scratch_shapes=[pltpu.VMEM((EZ * PITCH, NY), F32), pltpu.VMEM((SLOTS * BX, NY), F32)],
        compiler_params=params(24),
        name="forward",
    )(core, background, z_fwd, x_fwd, y_fwd, own, inside, outside)


def along_z_back(matrix, narrow, wide):
    def one(view, carry):
        for first in range(0, BX, AT_ONCE):
            columns = range(first, first + AT_ONCE)
            loaded = [
                narrow[pl.ds(pl.multiple_of((view * BX + c) * BZ, BZ), BZ), :] for c in columns
            ]
            product = dot(matrix[view], jnp.concatenate([terms(v) for v in loaded], axis=1))
            for i, column in enumerate(columns):
                wide[pl.ds(view * BX + column, EZ, stride=PITCH), :] = product[
                    :, i * NY : (i + 1) * NY
                ]
        return carry

    lax.fori_loop(0, VIEWS, one, 0)


def along_x_back(matrix, wide, pieces, starts):
    matrix = matrix[...]
    for piece, start in zip(pieces, starts):
        for first in range(0, BZ, AT_ONCE):
            planes = range(first, first + AT_ONCE)
            loaded = [
                wide[pl.ds(pl.multiple_of((start + p) * PITCH, 8), VU), :] for p in planes
            ]
            product = dot(matrix, jnp.concatenate([terms(v) for v in loaded], axis=1))
            for i, plane in enumerate(planes):
                piece[plane] = product[:, i * NY : (i + 1) * NY]


def back_steps(core, z_back, x_back, y_back, data, blur, own, inside, outside, wide, narrow):
    for view in range(VIEWS):
        lines = [
            data[pl.ds((view * BX + column) * LINE, BZ), :] for column in range(BX)
        ]
        ratio = jnp.concatenate(lines, axis=0) / blur[rows_of(view), :]
        narrow[rows_of(view), :] = along_y(y_back[view], ratio)
    along_z_back(z_back, narrow, wide)
    along_x_back(x_back, wide, [own, inside, outside], placed(core[0]))


def first_back_kernel(
    core, z_back, x_back, y_back, got, blur, data, own, inside, outside,
    wide, narrow, names, slots, sem,
):
    names[...] = got[pl.ds(SEND * BX, PEERS, stride=CHUNK), :].astype(jnp.int32)
    copy = pltpu.make_async_copy(names, slots, sem)
    copy.start()
    copy.wait()

    def unpack(peer, carry):
        for rank in range(SEND):
            slot = slots[peer, rank]
            start = (slot // BZ) * (BX * LINE) + slot % BZ
            data[pl.ds(start, BX, stride=LINE), :] = got[pl.ds(peer * CHUNK + rank * BX, BX), :]
        return carry

    lax.fori_loop(0, PEERS, unpack, 0, unroll=4)
    back_steps(core, z_back, x_back, y_back, data, blur, own, inside, outside, wide, narrow)


def first_back(core, z_back, x_back, y_back, got, blur):
    return pl.pallas_call(
        first_back_kernel,
        out_shape=[shape(((VIEWS + 1) * BX * LINE, NY))] + [shape((BZ, EX, NY))] * 3,
        in_specs=[SMEM] + [VMEM] * 5,
        out_specs=[VMEM] * 4,
        scratch_shapes=[
            pltpu.VMEM((EZ * PITCH, NY), F32),
            pltpu.VMEM((SLOTS * BX, NY), F32),
            pltpu.VMEM((PEERS, NY), jnp.int32),
            pltpu.SMEM((PEERS, NY), jnp.int32),
            pltpu.SemaphoreType.DMA,
        ],
        compiler_params=params(24),
        name="first_back",
    )(core, z_back, x_back, y_back, got, blur)


def later_kernel(
    core, background, z_fwd, x_fwd, y_fwd, z_back, x_back, y_back, e_own, e_inside, e_outside,
    data, own, inside, outside, wide, narrow, blur,
):
    forward_kernel(
        core, background, z_fwd, x_fwd, y_fwd, e_own, e_inside, e_outside, blur, wide, narrow
    )
    back_steps(core, z_back, x_back, y_back, data, blur, own, inside, outside, wide, narrow)


def later(core, background, forth, back, pieces, data):
    return pl.pallas_call(
        later_kernel,
        out_shape=[shape((BZ, EX, NY))] * 3,
        in_specs=[SMEM] * 2 + [VMEM] * 10,
        out_specs=[VMEM] * 3,
        scratch_shapes=[
            pltpu.VMEM((EZ * PITCH, NY), F32),
            pltpu.VMEM((SLOTS * BX, NY), F32),
            pltpu.VMEM((SLOTS * BX, NY), F32),
        ],
        compiler_params=params(24),
        name="forward_and_back",
    )(core, background, *forth, *back, *pieces, data)


def swaps(first, count):
    pairs = [(i, i + 1) for i in range(first, count - 1, 2)]
    return pairs + [(j, i) for i, j in pairs]


def beside(block):
    return lax.ppermute(block, "xy", swaps(0, PEERS)), lax.ppermute(block, "xy", swaps(1, PEERS))


def gathered(block, even_pair, odd_pair, odd):
    left = jnp.where(odd, even_pair, odd_pair)
    right = jnp.where(odd, odd_pair, even_pair)
    own = jnp.concatenate([left, block, right], axis=1)
    count = lax.axis_size("gz")
    return own, lax.ppermute(own, "gz", swaps(0, count)), lax.ppermute(own, "gz", swaps(1, count))


def scattered(own, inside, outside, odd):
    count = lax.axis_size("gz")
    total = (
        own
        + lax.ppermute(outside, "gz", swaps(1, count))
        + lax.ppermute(inside, "gz", swaps(0, count))
    )
    left, right = total[:, :R], total[:, R + BX :]
    even_pair = lax.ppermute(jnp.where(odd, left, right), "xy", swaps(0, PEERS))
    odd_pair = lax.ppermute(jnp.where(odd, right, left), "xy", swaps(1, PEERS))
    return total[:, R : R + BX] + even_pair + odd_pair


def local(
    tile_planes,
    plane_owner,
    plane_slot,
    view_shift,
    psf_z,
    psf_x,
    psf_y,
    background,
    initial_estimate,
):
    core = lax.rem(lax.axis_index("gz"), 2).astype(jnp.int32).reshape(1)
    odd = lax.rem(lax.axis_index("xy"), 2) == 1
    send = pack(plane_owner.reshape(SRC), plane_slot.reshape(SRC), tile_planes[0])
    send, *sides = lax.optimization_barrier((send, *beside(initial_estimate)))
    got = lax.all_to_all(
        send.reshape(PEERS, 1, CHUNK * NY), "xy", split_axis=0, concat_axis=0, tiled=True
    ).reshape(PEERS * CHUNK, NY)
    psf = jnp.concatenate([psf_z, psf_x, psf_y], axis=0)
    taps = psf / jnp.sum(psf, axis=1, keepdims=True)
    matrices = weights(taps, view_shift)
    forth, back = matrices[::2], matrices[1::2]
    estimate = initial_estimate
    for step in range(ITERS):
        if step:
            sides = beside(estimate)
        pieces = gathered(estimate, *sides, odd)
        if step == 0:
            blur = forward(core, background, *forth, *pieces)
            data, *parts = first_back(core, *back, got, blur)
        else:
            parts = later(core, background, forth, back, pieces, data)
        estimate = estimate * (scattered(*parts, odd) / VIEWS)
    return estimate


def solution(mesh):
    return jax.shard_map(
        local,
        mesh=mesh,
        in_specs=(
            P("gz", "xy", None),
            P("gz", "xy", None),
            P("gz", "xy"),
            P(),
            P(),
            P(),
            P(),
            P(),
            P("gz", "xy", None),
        ),
        out_specs=P("gz", "xy", None),
        check_vma=False,
    )
```

```python
import jax
import jax.numpy as jnp
from jax import lax
from jax.experimental import pallas as pl
from jax.experimental.pallas import tpu as pltpu
from jax.sharding import PartitionSpec as P

ITERS = 2
VIEWS = 6
TAPS = 33
R = 16
BZ = 16
BX = 16
NY = 128
SEND = 3
SRC = 96
PEERS = 64
EX = BX + 2 * R
EZ = BZ + 2 * R
SLOTS = VIEWS * BZ
CHUNK = SEND * BX + 1
VU = VIEWS * BX
PITCH = VU + 8
LINE = BX + 8
AT_ONCE = 4
F32 = jnp.float32
BF16 = jnp.bfloat16

VMEM = pl.BlockSpec(memory_space=pltpu.VMEM)
SMEM = pl.BlockSpec(memory_space=pltpu.SMEM)


def params(mib):
    return pltpu.CompilerParams(vmem_limit_bytes=mib * 1024 * 1024)


def shape(dims, dtype=F32):
    return jax.ShapeDtypeStruct(dims, dtype)


def split(value):
    high = value.astype(BF16)
    return high, (value - high.astype(F32)).astype(BF16)


def pack_kernel(named, planes, send, rows, count):
    for peer in range(PEERS):
        count[peer] = 0
    send[pl.ds(SEND * BX, PEERS, stride=CHUNK), :] = jnp.full((PEERS, NY), SLOTS, F32)
    for group in range(SRC // 8):
        for column in range(BX):
            rows[pl.ds(group * 8 * BX + column, 8, stride=BX), :] = planes[
                group * 8 : group * 8 + 8, column * NY : (column + 1) * NY
            ]
    lane = lax.broadcasted_iota(jnp.int32, (1, NY), 1)

    def place(plane, carry):
        peer = named[plane] >> 7
        rank = count[peer]
        count[peer] = rank + 1
        start = peer * CHUNK
        send[pl.ds(start + rank * BX, BX), :] = rows[pl.ds(pl.multiple_of(plane * BX, BX), BX), :]
        pltpu.store(
            send.at[pl.ds(start + SEND * BX, 1), :],
            jnp.full((1, NY), named[plane] & (NY - 1), jnp.int32).astype(F32),
            mask=lane == rank,
        )
        return carry

    lax.fori_loop(0, SRC, place, 0, unroll=8)


def pack(named, planes):
    return pl.pallas_call(
        pack_kernel,
        out_shape=shape((PEERS * CHUNK, NY)),
        in_specs=[SMEM, VMEM],
        out_specs=VMEM,
        scratch_shapes=[
            pltpu.VMEM((SRC * BX, NY), F32),
            pltpu.SMEM((PEERS,), jnp.int32),
        ],
        compiler_params=params(16),
        name="pack_planes",
    )(named, planes)


def bands(taps, first, place):
    row = lax.broadcasted_iota(jnp.int32, (BX, NY), 0)
    lane = place(lax.broadcasted_iota(jnp.int32, (BX, NY), 1))
    each = []
    for view in range(VIEWS):
        band = jnp.zeros((BX, NY), F32)
        for tap in range(TAPS):
            band = jnp.where(lane - row == tap, taps[first + view, tap], band)
        each.append(band)
    return jnp.concatenate(each + [jnp.zeros((NY - VU, NY), F32)], axis=0)


def by_terms(value):
    high, low = split(value)
    return jnp.concatenate([high, low, high], axis=1)


def views_of(ref):
    z_rows, x_rows = VIEWS * EZ, 3 * EX
    return (
        ref.at[pl.ds(0, z_rows), :],
        ref.at[pl.ds(z_rows, x_rows), :],
        ref.at[pl.ds(z_rows + x_rows, VIEWS * 3 * NY), :],
    )


def weight_kernel(index, taps, shift, z_fwd, x_fwd, y_fwd, back):
    z_back, x_back, y_back = views_of(back)
    band = bands(taps, 0, lambda lane: lane)
    turned = jnp.transpose(band)[:EZ]
    for view in range(VIEWS):
        z_fwd[view] = by_terms(band[view * BZ : (view + 1) * BZ, :EZ])
        z_back[pl.ds(view * EZ, EZ), : 3 * BZ] = by_terms(turned[:, view * BZ : (view + 1) * BZ])
    flip = jnp.where(index[0] % 2 == 0, 2 * BX, 0)
    band = bands(
        taps,
        VIEWS,
        lambda lane: jnp.where(
            lane < BX, lane + flip, jnp.where((lane >= 2 * BX) & (lane < EX), lane - flip, lane)
        ),
    )
    x_fwd[...] = by_terms(band[:VU, :EX])
    high, low = split(jnp.transpose(band)[:EX, :VU])
    for i, part in enumerate([high, low, high]):
        x_back[pl.ds(i * EX, EX), :VU] = part
    row = lax.broadcasted_iota(jnp.int32, (NY, NY), 0)
    lane = lax.broadcasted_iota(jnp.int32, (NY, NY), 1)

    def along_y(view, carry):
        offset = lane - row + R + shift[view]
        back = jnp.zeros((NY, NY), F32)
        for tap in range(TAPS):
            back = jnp.where(offset == tap, taps[2 * VIEWS + view, tap], back)
        high, low = split(back)
        y_back[pl.ds(pl.multiple_of(view * 3 * NY, NY), 3 * NY), :] = jnp.concatenate(
            [high, low, high], axis=0
        )
        high, low = split(jnp.transpose(back))
        y_fwd[view] = jnp.concatenate([high, low, high], axis=0)
        return carry

    lax.fori_loop(0, VIEWS, along_y, 0)


def weights(index, taps, shift):
    return pl.pallas_call(
        weight_kernel,
        out_shape=[
            shape((VIEWS, BZ, 3 * EZ), BF16),
            shape((VU, 3 * EX), BF16),
            shape((VIEWS, 3 * NY, NY), BF16),
            shape((VIEWS * EZ + 3 * EX + VIEWS * 3 * NY, NY), BF16),
        ],
        in_specs=[SMEM] * 3,
        out_specs=[VMEM] * 4,
        compiler_params=params(16),
        name="operator_matrices",
    )(index, taps, shift)


def dot(left, right):
    return jnp.dot(left, right, preferred_element_type=F32)


def terms(value):
    high, low = split(value)
    return jnp.concatenate([high, high, low], axis=0)


def along_x_fwd(matrix, pieces, starts, wide):
    matrix = matrix[...]
    for piece, start in zip(pieces, starts):
        for first in range(0, BZ, AT_ONCE):
            planes = range(first, first + AT_ONCE)
            product = dot(matrix, jnp.concatenate([terms(piece[p]) for p in planes], axis=1))
            for i, plane in enumerate(planes):
                rows = pl.ds(pl.multiple_of((start + plane) * PITCH, 8), VU)
                wide[rows, :] = product[:, i * NY : (i + 1) * NY]


def along_z_fwd(matrix, wide, narrow):
    def one(view, carry):
        for first in range(0, BX, AT_ONCE):
            columns = range(first, first + AT_ONCE)
            loaded = [wide[pl.ds(view * BX + c, EZ, stride=PITCH), :] for c in columns]
            product = dot(matrix[view], jnp.concatenate([terms(v) for v in loaded], axis=1))
            for i, column in enumerate(columns):
                rows = pl.ds(view * BZ * LINE + column, BZ, stride=LINE)
                narrow[rows, :] = product[:, i * NY : (i + 1) * NY]
        return carry

    lax.fori_loop(0, VIEWS, one, 0, unroll=True)


def rows_of(view):
    return pl.ds(view * BZ * BX, BZ * BX)


def planes_of(view):
    starts = [(view * BZ + plane) * LINE for plane in range(BZ)]
    return [pl.ds(start, BX) for start in starts]


def along_y(matrix, value):
    high, low = split(value)
    return dot(jnp.concatenate([high, high, low], axis=1), matrix)


def placed(core):
    inside = jnp.where(core == 0, 2 * R, 0)
    outside = jnp.where(core == 0, 0, 2 * R)
    return [R, inside, outside]


def forward_kernel(
    core, background, z_fwd, x_fwd, y_fwd, own, inside, outside, blur, wide, narrow
):
    along_x_fwd(x_fwd, [own, inside, outside], placed(core[0]), wide)
    along_z_fwd(z_fwd, wide, narrow)
    for view in range(VIEWS):
        value = jnp.concatenate([narrow[rows, :] for rows in planes_of(view)], axis=0)
        blur[rows_of(view), :] = along_y(y_fwd[view], value) + background[view]


def forward(core, background, z_fwd, x_fwd, y_fwd, own, inside, outside):
    return pl.pallas_call(
        forward_kernel,
        out_shape=shape((SLOTS * BX, NY)),
        in_specs=[SMEM] * 2 + [VMEM] * 6,
        out_specs=VMEM,
        scratch_shapes=[pltpu.VMEM((EZ * PITCH, NY), F32), pltpu.VMEM((SLOTS * LINE, NY), F32)],
        compiler_params=params(24),
        name="forward",
    )(core, background, z_fwd, x_fwd, y_fwd, own, inside, outside)


def along_z_back(matrix, narrow, wide):
    def one(view, carry):
        for first in range(0, BX, AT_ONCE):
            columns = range(first, first + AT_ONCE)
            loaded = [
                narrow[pl.ds(view * BZ * LINE + c, BZ, stride=LINE), :] for c in columns
            ]
            rows = pl.ds(pl.multiple_of(view * EZ, EZ), EZ)
            product = dot(
                matrix[rows, : 3 * BZ], jnp.concatenate([terms(v) for v in loaded], axis=1)
            )
            for i, column in enumerate(columns):
                wide[pl.ds(view * BX + column, EZ, stride=PITCH), :] = product[
                    :, i * NY : (i + 1) * NY
                ]
        return carry

    lax.fori_loop(0, VIEWS, one, 0, unroll=True)


def along_x_back(matrix, wide, pieces, starts):
    parts = [matrix[pl.ds(i * EX, EX), :VU] for i in range(3)]
    matrix = jnp.concatenate(parts, axis=1)
    for piece, start in zip(pieces, starts):
        for first in range(0, BZ, AT_ONCE):
            planes = range(first, first + AT_ONCE)
            loaded = [
                wide[pl.ds(pl.multiple_of((start + p) * PITCH, 8), VU), :] for p in planes
            ]
            product = dot(matrix, jnp.concatenate([terms(v) for v in loaded], axis=1))
            for i, plane in enumerate(planes):
                piece[plane] = product[:, i * NY : (i + 1) * NY]


def back_steps(core, where, back, got, blur, own, inside, outside, wide, narrow):
    z_back, x_back, y_back = views_of(back)
    for view in range(VIEWS):
        data = [got[pl.ds(where[view * BZ + plane], BX), :] for plane in range(BZ)]
        ratio = jnp.concatenate(data, axis=0) / blur[rows_of(view), :]
        value = along_y(y_back[pl.ds(view * 3 * NY, 3 * NY), :], ratio)
        for plane, rows in enumerate(planes_of(view)):
            narrow[rows, :] = value[plane * BX : (plane + 1) * BX]
    along_z_back(z_back, narrow, wide)
    along_x_back(x_back, wide, [own, inside, outside], placed(core[0]))


def first_back_kernel(
    core, back, got, blur, where, own, inside, outside,
    wide, narrow, names, slots, sem,
):
    named = got[pl.ds(SEND * BX, PEERS, stride=CHUNK), :].astype(jnp.int32)
    names[...] = jnp.transpose(jnp.concatenate([named, named], axis=0))[:8]
    copy = pltpu.make_async_copy(names, slots, sem)
    copy.start()
    copy.wait()
    for peer in range(PEERS):
        for rank in range(SEND):
            where[slots[rank, peer]] = peer * CHUNK + rank * BX
    back_steps(core, where, back, got, blur, own, inside, outside, wide, narrow)


def first_back(core, back, got, blur):
    return pl.pallas_call(
        first_back_kernel,
        out_shape=[shape((NY,), jnp.int32)] + [shape((BZ, EX, NY))] * 3,
        in_specs=[SMEM] + [VMEM] * 3,
        out_specs=[SMEM] + [VMEM] * 3,
        scratch_shapes=[
            pltpu.VMEM((EZ * PITCH, NY), F32),
            pltpu.VMEM((SLOTS * LINE, NY), F32),
            pltpu.VMEM((8, NY), jnp.int32),
            pltpu.SMEM((8, NY), jnp.int32),
            pltpu.SemaphoreType.DMA,
        ],
        compiler_params=params(24),
        name="first_back",
    )(core, back, got, blur)


def later_kernel(
    core, background, where, z_fwd, x_fwd, y_fwd, back,
    e_own, e_inside, e_outside, got, own, inside, outside, wide, narrow, blur,
):
    forward_kernel(
        core, background, z_fwd, x_fwd, y_fwd, e_own, e_inside, e_outside, blur, wide, narrow
    )
    back_steps(core, where, back, got, blur, own, inside, outside, wide, narrow)


def later(core, background, where, forth, back, pieces, got):
    return pl.pallas_call(
        later_kernel,
        out_shape=[shape((BZ, EX, NY))] * 3,
        in_specs=[SMEM] * 3 + [VMEM] * 8,
        out_specs=[VMEM] * 3,
        scratch_shapes=[
            pltpu.VMEM((EZ * PITCH, NY), F32),
            pltpu.VMEM((SLOTS * LINE, NY), F32),
            pltpu.VMEM((SLOTS * BX, NY), F32),
        ],
        compiler_params=params(24),
        name="forward_and_back",
    )(core, background, where, *forth, back, *pieces, got)


def swaps(first, count):
    pairs = [(i, i + 1) for i in range(first, count - 1, 2)]
    return pairs + [(j, i) for i, j in pairs]


def to_partners(to_even, to_odd):
    return lax.ppermute(to_even, "xy", swaps(0, PEERS)), lax.ppermute(to_odd, "xy", swaps(1, PEERS))


def past_partners(past_even, past_odd):
    right = [(i, i + 2) for i in range(PEERS - 2)]
    one = [p for p in right if p[0] % 2 == 0] + [(j, i) for i, j in right if i % 2 == 1]
    two = [(j, i) for i, j in one]
    return lax.ppermute(past_even, "xy", one), lax.ppermute(past_odd, "xy", two)


def above_and_below(block):
    count = lax.axis_size("gz")
    return lax.ppermute(block, "gz", swaps(0, count)), lax.ppermute(block, "gz", swaps(1, count))


def slab_sum(own, inside, outside):
    count = lax.axis_size("gz")
    return (
        own
        + lax.ppermute(outside, "gz", swaps(1, count))
        + lax.ppermute(inside, "gz", swaps(0, count))
    )


def three_sums(total):
    even, odd = to_partners(total[:, : 2 * BX], total[:, BX:])
    behind_odd, behind_even = past_partners(total[:, :BX], total[:, 2 * BX :])
    return jnp.concatenate(
        [
            total[:, :BX] + even[:, BX:] + behind_even,
            total[:, BX : 2 * BX] + even[:, :BX] + odd[:, BX:],
            total[:, 2 * BX :] + odd[:, :BX] + behind_odd,
        ],
        axis=1,
    )


def own_sum(total):
    even, odd = to_partners(total[:, :BX], total[:, 2 * BX :])
    return total[:, BX : 2 * BX] + even + odd


def local(
    tile_planes,
    plane_owner,
    plane_slot,
    view_shift,
    psf_z,
    psf_x,
    psf_y,
    background,
    initial_estimate,
):
    core = lax.rem(lax.axis_index("gz"), 2).astype(jnp.int32).reshape(1)
    index = lax.axis_index("xy").astype(jnp.int32).reshape(1)
    send = pack(plane_owner.reshape(SRC) * NY + plane_slot.reshape(SRC), tile_planes[0])
    even, odd = to_partners(initial_estimate, initial_estimate)
    send, even, odd = lax.optimization_barrier((send, even, odd))
    got = lax.all_to_all(
        send.reshape(PEERS, 1, CHUNK * NY), "xy", split_axis=0, concat_axis=0, tiled=True
    ).reshape(PEERS * CHUNK, NY)
    psf = jnp.concatenate([psf_z, psf_x, psf_y], axis=0)
    taps = psf / jnp.sum(psf, axis=1, keepdims=True)
    *forth, back = weights(index, taps, view_shift)
    bricks = jnp.concatenate([even, initial_estimate, odd], axis=1)
    for step in range(ITERS):
        pieces = (bricks, *above_and_below(bricks))
        if step == 0:
            blur = forward(core, background, *forth, *pieces)
            where, *parts = first_back(core, back, got, blur)
        else:
            parts = later(core, background, where, forth, back, pieces, got)
        total = slab_sum(*parts)
        if step + 1 < ITERS:
            bricks = bricks * (three_sums(total) / VIEWS)
    return bricks[:, BX : 2 * BX] * (own_sum(total) / VIEWS)


def solution(mesh):
    return jax.shard_map(
        local,
        mesh=mesh,
        in_specs=(
            P("gz", "xy", None),
            P("gz", "xy", None),
            P("gz", "xy"),
            P(),
            P(),
            P(),
            P(),
            P(),
            P("gz", "xy", None),
        ),
        out_specs=P("gz", "xy", None),
        check_vma=False,
    )
```

```python
import jax
import jax.numpy as jnp
from jax import lax
from jax.experimental import pallas as pl
from jax.experimental.pallas import tpu as pltpu
from jax.sharding import PartitionSpec as P

ITERS = 2
VIEWS = 6
TAPS = 33
R = 16
BZ = 16
BX = 16
NY = 128
SEND = 3
SRC = 96
PEERS = 64
EX = BX + 2 * R
EZ = BZ + 2 * R
SLOTS = VIEWS * BZ
CHUNK = SEND * BX + 1
VU = VIEWS * BX
PITCH = VU + 8
LINE = BX + 8
AT_ONCE = 4
F32 = jnp.float32
BF16 = jnp.bfloat16

VMEM = pl.BlockSpec(memory_space=pltpu.VMEM)
SMEM = pl.BlockSpec(memory_space=pltpu.SMEM)


def params(mib):
    return pltpu.CompilerParams(vmem_limit_bytes=mib * 1024 * 1024)


def shape(dims, dtype=F32):
    return jax.ShapeDtypeStruct(dims, dtype)


def split(value):
    high = value.astype(BF16)
    return high, (value - high.astype(F32)).astype(BF16)


def pack_kernel(named, planes, send, rows, count):
    for peer in range(PEERS):
        count[peer] = 0
    send[pl.ds(SEND * BX, PEERS, stride=CHUNK), :] = jnp.full((PEERS, NY), SLOTS, F32)
    for group in range(SRC // 8):
        for column in range(BX):
            rows[pl.ds(group * 8 * LINE + column, 8, stride=LINE), :] = planes[
                group * 8 : group * 8 + 8, column * NY : (column + 1) * NY
            ]
    lane = lax.broadcasted_iota(jnp.int32, (1, NY), 1)

    def place(plane, carry):
        peer = named[plane] >> 7
        rank = count[peer]
        count[peer] = rank + 1
        start = peer * CHUNK
        send[pl.ds(start + rank * BX, BX), :] = rows[pl.ds(pl.multiple_of(plane * LINE, 8), BX), :]
        pltpu.store(
            send.at[pl.ds(start + SEND * BX, 1), :],
            jnp.full((1, NY), named[plane] & (NY - 1), jnp.int32).astype(F32),
            mask=lane == rank,
        )
        return carry

    lax.fori_loop(0, SRC, place, 0, unroll=8)


def pack(named, planes):
    return pl.pallas_call(
        pack_kernel,
        out_shape=shape((PEERS * CHUNK, NY)),
        in_specs=[SMEM, VMEM],
        out_specs=VMEM,
        scratch_shapes=[
            pltpu.VMEM((SRC * LINE, NY), F32),
            pltpu.SMEM((PEERS,), jnp.int32),
        ],
        compiler_params=params(16),
        name="pack_planes",
    )(named, planes)


def bands(taps, first, place):
    row = lax.broadcasted_iota(jnp.int32, (BX, NY), 0)
    lane = place(lax.broadcasted_iota(jnp.int32, (BX, NY), 1))
    each = []
    for view in range(VIEWS):
        band = jnp.zeros((BX, NY), F32)
        for tap in range(TAPS):
            band = jnp.where(lane - row == tap, taps[first + view, tap], band)
        each.append(band)
    return jnp.concatenate(each + [jnp.zeros((NY - VU, NY), F32)], axis=0)


def by_terms(value):
    high, low = split(value)
    return jnp.concatenate([high, low, high], axis=1)


def views_of(ref):
    z_rows, x_rows = VIEWS * EZ, 2 * EX
    return (
        ref.at[pl.ds(0, z_rows), :],
        ref.at[pl.ds(z_rows, x_rows), :],
        ref.at[pl.ds(z_rows + x_rows, VIEWS * 3 * NY), :],
    )


def weight_kernel(index, taps, shift, z_fwd, x_fwd, y_fwd, back):
    z_back, x_back, y_back = views_of(back)
    band = bands(taps, 0, lambda lane: lane)
    turned = jnp.transpose(band)[:EZ]
    for view in range(VIEWS):
        z_fwd[view] = by_rows(band[view * BZ : (view + 1) * BZ, :EZ])
        z_back[pl.ds(view * EZ, EZ), : 3 * BZ] = by_terms(turned[:, view * BZ : (view + 1) * BZ])
    flip = jnp.where(index[0] % 2 == 0, 2 * BX, 0)
    band = bands(
        taps,
        VIEWS,
        lambda lane: jnp.where(
            lane < BX, lane + flip, jnp.where((lane >= 2 * BX) & (lane < EX), lane - flip, lane)
        ),
    )
    x_fwd[...] = by_terms(band[:VU, :EX])
    high, low = split(jnp.transpose(band)[:EX, :VU])
    for i, part in enumerate([high, low]):
        x_back[pl.ds(i * EX, EX), :VU] = part
    row = lax.broadcasted_iota(jnp.int32, (NY, NY), 0)
    lane = lax.broadcasted_iota(jnp.int32, (NY, NY), 1)

    def along_y(view, carry):
        offset = lane - row + R + shift[view]
        back = jnp.zeros((NY, NY), F32)
        for tap in range(TAPS):
            back = jnp.where(offset == tap, taps[2 * VIEWS + view, tap], back)
        high, low = split(back)
        y_back[pl.ds(pl.multiple_of(view * 3 * NY, NY), 3 * NY), :] = jnp.concatenate(
            [high, low, high], axis=0
        )
        high, low = split(jnp.transpose(back))
        y_fwd[view] = jnp.concatenate([high, low, high], axis=0)
        return carry

    lax.fori_loop(0, VIEWS, along_y, 0)


def weights(index, taps, shift):
    return pl.pallas_call(
        weight_kernel,
        out_shape=[
            shape((VIEWS, 2 * BZ, 2 * EZ), BF16),
            shape((VU, 3 * EX), BF16),
            shape((VIEWS, 3 * NY, NY), BF16),
            shape((VIEWS * EZ + 2 * EX + VIEWS * 3 * NY, NY), BF16),
        ],
        in_specs=[SMEM] * 3,
        out_specs=[VMEM] * 4,
        compiler_params=params(16),
        name="operator_matrices",
    )(index, taps, shift)


def dot(left, right):
    return jnp.dot(left, right, preferred_element_type=F32)


def by_rows(value):
    high, low = split(value)
    upper = jnp.concatenate([high, high], axis=1)
    return jnp.concatenate([upper, jnp.concatenate([low, jnp.zeros_like(low)], axis=1)], axis=0)


def dot_by_rows(matrix, values):
    pairs = [jnp.concatenate(split(value), axis=0) for value in values]
    product = dot(matrix, jnp.concatenate(pairs, axis=1))
    half = product.shape[0] // 2
    return product[:half] + product[half:]


def terms(value):
    high, low = split(value)
    return jnp.concatenate([high, high, low], axis=0)


def along_x_fwd(matrix, pieces, starts, wide):
    matrix = matrix[...]
    for piece, start in zip(pieces, starts):
        for first in range(0, BZ, AT_ONCE):
            planes = range(first, first + AT_ONCE)
            product = dot(matrix, jnp.concatenate([terms(piece[p]) for p in planes], axis=1))
            for i, plane in enumerate(planes):
                rows = pl.ds(pl.multiple_of((start + plane) * PITCH, 8), VU)
                wide[rows, :] = product[:, i * NY : (i + 1) * NY]


def along_z_fwd(matrix, wide, narrow):
    def one(view, carry):
        for first in range(0, BX, AT_ONCE):
            columns = range(first, first + AT_ONCE)
            loaded = [wide[pl.ds(view * BX + c, EZ, stride=PITCH), :] for c in columns]
            product = dot_by_rows(matrix[view], loaded)
            for i, column in enumerate(columns):
                rows = pl.ds(view * BZ * LINE + column, BZ, stride=LINE)
                narrow[rows, :] = product[:, i * NY : (i + 1) * NY]
        return carry

    lax.fori_loop(0, VIEWS, one, 0, unroll=True)


def rows_of(view):
    return pl.ds(view * BZ * BX, BZ * BX)


def planes_of(view):
    starts = [(view * BZ + plane) * LINE for plane in range(BZ)]
    return [pl.ds(start, BX) for start in starts]


def along_y(matrix, value):
    high, low = split(value)
    return dot(jnp.concatenate([high, high, low], axis=1), matrix)


def placed():
    core = lax.rem(lax.axis_index("gz"), 2)
    inside = jnp.where(core == 0, 2 * R, 0)
    outside = jnp.where(core == 0, 0, 2 * R)
    return [R, inside, outside]


def forward_kernel(
    background, z_fwd, x_fwd, y_fwd, own, inside, outside, blur, wide, narrow
):
    along_x_fwd(x_fwd, [own, inside, outside], placed(), wide)
    along_z_fwd(z_fwd, wide, narrow)
    for view in range(VIEWS):
        value = jnp.concatenate([narrow[rows, :] for rows in planes_of(view)], axis=0)
        blur[rows_of(view), :] = along_y(y_fwd[view], value) + background[view : view + 1, :]


def forward(background, z_fwd, x_fwd, y_fwd, own, inside, outside):
    return pl.pallas_call(
        forward_kernel,
        out_shape=shape((SLOTS * BX, NY)),
        in_specs=[VMEM] * 7,
        out_specs=VMEM,
        scratch_shapes=[pltpu.VMEM((EZ * PITCH, NY), F32), pltpu.VMEM((SLOTS * LINE, NY), F32)],
        compiler_params=params(24),
        name="forward",
    )(background, z_fwd, x_fwd, y_fwd, own, inside, outside)


def along_z_back(matrix, narrow, wide):
    def one(view, carry):
        for first in range(0, BX, AT_ONCE):
            columns = range(first, first + AT_ONCE)
            loaded = [
                narrow[pl.ds(view * BZ * LINE + c, BZ, stride=LINE), :] for c in columns
            ]
            rows = pl.ds(pl.multiple_of(view * EZ, EZ), EZ)
            product = dot(
                matrix[rows, : 3 * BZ], jnp.concatenate([terms(v) for v in loaded], axis=1)
            )
            for i, column in enumerate(columns):
                wide[pl.ds(view * BX + column, EZ, stride=PITCH), :] = product[
                    :, i * NY : (i + 1) * NY
                ]
        return carry

    lax.fori_loop(0, VIEWS, one, 0, unroll=True)


def along_x_back(matrix, wide, pieces, starts):
    high, low = [matrix[pl.ds(i * EX, EX), :VU] for i in range(2)]
    upper = jnp.concatenate([high, high], axis=1)
    lower = jnp.concatenate([low, jnp.zeros_like(low)], axis=1)
    matrix = jnp.concatenate([upper, lower], axis=0)
    for piece, start in zip(pieces, starts):
        for first in range(0, BZ, AT_ONCE):
            planes = range(first, first + AT_ONCE)
            loaded = [
                wide[pl.ds(pl.multiple_of((start + p) * PITCH, 8), VU), :] for p in planes
            ]
            product = dot_by_rows(matrix, loaded)
            for i, plane in enumerate(planes):
                piece[plane] = product[:, i * NY : (i + 1) * NY]


def back_steps(where, back, got, blur, own, inside, outside, wide, narrow):
    z_back, x_back, y_back = views_of(back)
    for view in range(VIEWS):
        data = [got[pl.ds(where[view * BZ + plane], BX), :] for plane in range(BZ)]
        ratio = jnp.concatenate(data, axis=0) / blur[rows_of(view), :]
        value = along_y(y_back[pl.ds(view * 3 * NY, 3 * NY), :], ratio)
        for plane, rows in enumerate(planes_of(view)):
            narrow[rows, :] = value[plane * BX : (plane + 1) * BX]
    along_z_back(z_back, narrow, wide)
    along_x_back(x_back, wide, [own, inside, outside], placed())


def slot_copy(got, names, slots, sem):
    named = got[pl.ds(SEND * BX, PEERS, stride=CHUNK), :].astype(jnp.int32)
    names[...] = jnp.transpose(jnp.concatenate([named, named], axis=0))[:8]
    return pltpu.make_async_copy(names, slots, sem)


def fill_table(slots, where):
    for peer in range(PEERS):
        for rank in range(SEND):
            where[slots[rank, peer]] = peer * CHUNK + rank * BX


SCRATCH = [
    pltpu.VMEM((EZ * PITCH, NY), F32),
    pltpu.VMEM((SLOTS * LINE, NY), F32),
    pltpu.VMEM((8, NY), jnp.int32),
    pltpu.SMEM((8, NY), jnp.int32),
    pltpu.SMEM((NY,), jnp.int32),
    pltpu.SemaphoreType.DMA,
]


def first_back_kernel(
    back, got, blur, own, inside, outside, wide, narrow, names, slots, where, sem
):
    copy = slot_copy(got, names, slots, sem)
    copy.start()
    copy.wait()
    fill_table(slots, where)
    back_steps(where, back, got, blur, own, inside, outside, wide, narrow)


def first_back(back, got, blur):
    return pl.pallas_call(
        first_back_kernel,
        out_shape=[shape((BZ, EX, NY))] * 3,
        in_specs=[VMEM] * 3,
        out_specs=[VMEM] * 3,
        scratch_shapes=SCRATCH,
        compiler_params=params(24),
        name="first_back",
    )(back, got, blur)


def later_kernel(
    background, z_fwd, x_fwd, y_fwd, back, e_own, e_inside, e_outside, got, own, inside, outside,
    wide, narrow, names, slots, where, sem, blur,
):
    copy = slot_copy(got, names, slots, sem)
    copy.start()
    forward_kernel(
        background, z_fwd, x_fwd, y_fwd, e_own, e_inside, e_outside, blur, wide, narrow
    )
    copy.wait()
    fill_table(slots, where)
    back_steps(where, back, got, blur, own, inside, outside, wide, narrow)


def later(background, forth, back, pieces, got):
    return pl.pallas_call(
        later_kernel,
        out_shape=[shape((BZ, EX, NY))] * 3,
        in_specs=[VMEM] * 9,
        out_specs=[VMEM] * 3,
        scratch_shapes=SCRATCH + [pltpu.VMEM((SLOTS * BX, NY), F32)],
        compiler_params=params(24),
        name="forward_and_back",
    )(background, *forth, back, *pieces, got)


def swaps(first, count):
    pairs = [(i, i + 1) for i in range(first, count - 1, 2)]
    return pairs + [(j, i) for i, j in pairs]


def to_partners(to_even, to_odd):
    return lax.ppermute(to_even, "xy", swaps(0, PEERS)), lax.ppermute(to_odd, "xy", swaps(1, PEERS))


def past_partners(past_even, past_odd):
    right = [(i, i + 2) for i in range(PEERS - 2)]
    one = [p for p in right if p[0] % 2 == 0] + [(j, i) for i, j in right if i % 2 == 1]
    two = [(j, i) for i, j in one]
    return lax.ppermute(past_even, "xy", one), lax.ppermute(past_odd, "xy", two)


def above_and_below(block):
    count = lax.axis_size("gz")
    return lax.ppermute(block, "gz", swaps(0, count)), lax.ppermute(block, "gz", swaps(1, count))


def slab_sum(own, inside, outside):
    count = lax.axis_size("gz")
    return (
        own
        + lax.ppermute(outside, "gz", swaps(1, count))
        + lax.ppermute(inside, "gz", swaps(0, count))
    )


def three_sums(total):
    even, odd = to_partners(total[:, : 2 * BX], total[:, BX:])
    behind_odd, behind_even = past_partners(total[:, :BX], total[:, 2 * BX :])
    return jnp.concatenate(
        [
            total[:, :BX] + even[:, BX:] + behind_even,
            total[:, BX : 2 * BX] + even[:, :BX] + odd[:, BX:],
            total[:, 2 * BX :] + odd[:, :BX] + behind_odd,
        ],
        axis=1,
    )


def own_sum(total):
    even, odd = to_partners(total[:, :BX], total[:, 2 * BX :])
    return total[:, BX : 2 * BX] + even + odd


def local(
    tile_planes,
    plane_owner,
    plane_slot,
    view_shift,
    psf_z,
    psf_x,
    psf_y,
    background,
    initial_estimate,
):
    index = lax.axis_index("xy").astype(jnp.int32).reshape(1)
    send = pack(plane_owner.reshape(SRC) * NY + plane_slot.reshape(SRC), tile_planes[0])
    even, odd = to_partners(initial_estimate, initial_estimate)
    send, even, odd = lax.optimization_barrier((send, even, odd))
    got = lax.all_to_all(
        send.reshape(PEERS, 1, CHUNK * NY), "xy", split_axis=0, concat_axis=0, tiled=True
    ).reshape(PEERS * CHUNK, NY)
    psf = jnp.concatenate([psf_z, psf_x, psf_y], axis=0)
    taps = psf / jnp.sum(psf, axis=1, keepdims=True)
    *forth, back = weights(index, taps, view_shift)
    levels = jnp.broadcast_to(background[:, None], (VIEWS, NY))
    bricks = jnp.concatenate([even, initial_estimate, odd], axis=1)
    for step in range(ITERS):
        pieces = (bricks, *above_and_below(bricks))
        if step == 0:
            blur = forward(levels, *forth, *pieces)
            parts = first_back(back, got, blur)
        else:
            parts = later(levels, forth, back, pieces, got)
        total = slab_sum(*parts)
        if step + 1 < ITERS:
            bricks = bricks * (three_sums(total) / VIEWS)
    return bricks[:, BX : 2 * BX] * (own_sum(total) / VIEWS)


def solution(mesh):
    return jax.shard_map(
        local,
        mesh=mesh,
        in_specs=(
            P("gz", "xy", None),
            P("gz", "xy", None),
            P("gz", "xy"),
            P(),
            P(),
            P(),
            P(),
            P(),
            P("gz", "xy", None),
        ),
        out_specs=P("gz", "xy", None),
        check_vma=False,
    )
```

```python
import jax
import jax.numpy as jnp
from jax import lax
from jax.experimental import pallas as pl
from jax.experimental.pallas import tpu as pltpu
from jax.sharding import PartitionSpec as P

ITERS = 2
VIEWS = 6
TAPS = 33
R = 16
BZ = 16
BX = 16
NY = 128
SEND = 3
SRC = 96
PEERS = 64
EX = BX + 2 * R
EZ = BZ + 2 * R
SLOTS = VIEWS * BZ
CHUNK = SEND * BX + 1
VU = VIEWS * BX
PITCH = VU + 8
LINE = BX + 8
AT_ONCE = 4
F32 = jnp.float32
BF16 = jnp.bfloat16

VMEM = pl.BlockSpec(memory_space=pltpu.VMEM)
SMEM = pl.BlockSpec(memory_space=pltpu.SMEM)


def params(mib):
    return pltpu.CompilerParams(vmem_limit_bytes=mib * 1024 * 1024)


def shape(dims, dtype=F32):
    return jax.ShapeDtypeStruct(dims, dtype)


def split(value):
    high = value.astype(BF16)
    return high, (value - high.astype(F32)).astype(BF16)


def pack_kernel(named_in, planes, send, rows, count, named, sem):
    copy = pltpu.make_async_copy(named_in, named, sem)
    copy.start()
    for peer in range(PEERS):
        count[peer] = 0
    send[pl.ds(SEND * BX, PEERS, stride=CHUNK), :] = jnp.full((PEERS, NY), SLOTS, F32)
    for group in range(SRC // 8):
        for column in range(BX):
            rows[pl.ds(group * 8 * LINE + column, 8, stride=LINE), :] = planes[
                group * 8 : group * 8 + 8, column * NY : (column + 1) * NY
            ]
    lane = lax.broadcasted_iota(jnp.int32, (1, NY), 1)
    copy.wait()

    def place(plane, carry):
        peer = named[0, plane] >> 7
        rank = count[peer]
        count[peer] = rank + 1
        start = peer * CHUNK
        send[pl.ds(start + rank * BX, BX), :] = rows[pl.ds(pl.multiple_of(plane * LINE, 8), BX), :]
        pltpu.store(
            send.at[pl.ds(start + SEND * BX, 1), :],
            jnp.full((1, NY), named[0, plane] & (NY - 1), jnp.int32).astype(F32),
            mask=lane == rank,
        )
        return carry

    lax.fori_loop(0, SRC, place, 0, unroll=8)


def pack(named, planes):
    return pl.pallas_call(
        pack_kernel,
        out_shape=shape((PEERS * CHUNK, NY)),
        in_specs=[VMEM, VMEM],
        out_specs=VMEM,
        scratch_shapes=[
            pltpu.VMEM((SRC * LINE, NY), F32),
            pltpu.SMEM((PEERS,), jnp.int32),
            pltpu.SMEM((1, NY), jnp.int32),
            pltpu.SemaphoreType.DMA,
        ],
        compiler_params=params(16),
        name="pack_planes",
    )(named, planes)


def bands(taps, first, place):
    row = lax.broadcasted_iota(jnp.int32, (BX, NY), 0)
    lane = place(lax.broadcasted_iota(jnp.int32, (BX, NY), 1))
    each = []
    for view in range(VIEWS):
        band = jnp.zeros((BX, NY), F32)
        for tap in range(TAPS):
            band = jnp.where(lane - row == tap, taps[first + view, tap], band)
        each.append(band)
    return jnp.concatenate(each + [jnp.zeros((NY - VU, NY), F32)], axis=0)


def by_terms(value):
    high, low = split(value)
    return jnp.concatenate([high, low, high], axis=1)


def views_of(ref):
    z_rows, x_rows = VIEWS * EZ, 3 * EX
    return (
        ref.at[pl.ds(0, z_rows), :],
        ref.at[pl.ds(z_rows, x_rows), :],
        ref.at[pl.ds(z_rows + x_rows, VIEWS * 3 * NY), :],
    )


def weight_kernel(index, taps, shift, z_fwd, x_fwd, y_fwd, back):
    z_back, x_back, y_back = views_of(back)
    band = bands(taps, 0, lambda lane: lane)
    turned = jnp.transpose(band)[:EZ]
    for view in range(VIEWS):
        z_fwd[view] = by_terms(band[view * BZ : (view + 1) * BZ, :EZ])
        z_back[pl.ds(view * EZ, EZ), : 3 * BZ] = by_terms(turned[:, view * BZ : (view + 1) * BZ])
    flip = jnp.where(index[0] % 2 == 0, 2 * BX, 0)
    band = bands(
        taps,
        VIEWS,
        lambda lane: jnp.where(
            lane < BX, lane + flip, jnp.where((lane >= 2 * BX) & (lane < EX), lane - flip, lane)
        ),
    )
    x_fwd[...] = by_terms(band[:VU, :EX])
    high, low = split(jnp.transpose(band)[:EX, :VU])
    for i, part in enumerate([high, low, high]):
        x_back[pl.ds(i * EX, EX), :VU] = part
    row = lax.broadcasted_iota(jnp.int32, (NY, NY), 0)
    lane = lax.broadcasted_iota(jnp.int32, (NY, NY), 1)

    def along_y(view, carry):
        offset = lane - row + R + shift[view]
        back = jnp.zeros((NY, NY), F32)
        for tap in range(TAPS):
            back = jnp.where(offset == tap, taps[2 * VIEWS + view, tap], back)
        high, low = split(back)
        y_back[pl.ds(pl.multiple_of(view * 3 * NY, NY), 3 * NY), :] = jnp.concatenate(
            [high, low, high], axis=0
        )
        high, low = split(jnp.transpose(back))
        y_fwd[view] = jnp.concatenate([high, low, high], axis=0)
        return carry

    lax.fori_loop(0, VIEWS, along_y, 0)


def weights(index, taps, shift):
    return pl.pallas_call(
        weight_kernel,
        out_shape=[
            shape((VIEWS, BZ, 3 * EZ), BF16),
            shape((VU, 3 * EX), BF16),
            shape((VIEWS, 3 * NY, NY), BF16),
            shape((VIEWS * EZ + 3 * EX + VIEWS * 3 * NY, NY), BF16),
        ],
        in_specs=[SMEM] * 3,
        out_specs=[VMEM] * 4,
        compiler_params=params(16),
        name="operator_matrices",
    )(index, taps, shift)


def dot(left, right):
    return jnp.dot(left, right, preferred_element_type=F32)


def terms(value):
    high, low = split(value)
    return jnp.concatenate([high, high, low], axis=0)


def along_x_fwd(matrix, pieces, starts, wide):
    matrix = matrix[...]
    for piece, start in zip(pieces, starts):
        for first in range(0, BZ, AT_ONCE):
            planes = range(first, first + AT_ONCE)
            product = dot(matrix, jnp.concatenate([terms(piece[p]) for p in planes], axis=1))
            for i, plane in enumerate(planes):
                rows = pl.ds(pl.multiple_of((start + plane) * PITCH, 8), VU)
                wide[rows, :] = product[:, i * NY : (i + 1) * NY]


def along_z_fwd(matrix, wide, narrow):
    def one(view, carry):
        for first in range(0, BX, AT_ONCE):
            columns = range(first, first + AT_ONCE)
            loaded = [wide[pl.ds(view * BX + c, EZ, stride=PITCH), :] for c in columns]
            product = dot(matrix[view], jnp.concatenate([terms(v) for v in loaded], axis=1))
            for i, column in enumerate(columns):
                rows = pl.ds(view * BZ * LINE + column, BZ, stride=LINE)
                narrow[rows, :] = product[:, i * NY : (i + 1) * NY]
        return carry

    lax.fori_loop(0, VIEWS, one, 0, unroll=True)


def rows_of(view):
    return pl.ds(view * BZ * BX, BZ * BX)


def planes_of(view):
    starts = [(view * BZ + plane) * LINE for plane in range(BZ)]
    return [pl.ds(start, BX) for start in starts]


def along_y(matrix, value):
    high, low = split(value)
    return dot(jnp.concatenate([high, high, low], axis=1), matrix)


def placed(core):
    inside = jnp.where(core == 0, 2 * R, 0)
    outside = jnp.where(core == 0, 0, 2 * R)
    return [R, inside, outside]


def forward_kernel(
    core, background, z_fwd, x_fwd, y_fwd, own, inside, outside, blur, wide, narrow
):
    along_x_fwd(x_fwd, [own, inside, outside], placed(core[0]), wide)
    along_z_fwd(z_fwd, wide, narrow)
    for view in range(VIEWS):
        value = jnp.concatenate([narrow[rows, :] for rows in planes_of(view)], axis=0)
        blur[rows_of(view), :] = along_y(y_fwd[view], value) + background[view]


def forward(core, background, z_fwd, x_fwd, y_fwd, own, inside, outside):
    return pl.pallas_call(
        forward_kernel,
        out_shape=shape((SLOTS * BX, NY)),
        in_specs=[SMEM] * 2 + [VMEM] * 6,
        out_specs=VMEM,
        scratch_shapes=[pltpu.VMEM((EZ * PITCH, NY), F32), pltpu.VMEM((SLOTS * LINE, NY), F32)],
        compiler_params=params(24),
        name="forward",
    )(core, background, z_fwd, x_fwd, y_fwd, own, inside, outside)


def along_z_back(matrix, narrow, wide):
    def one(view, carry):
        for first in range(0, BX, AT_ONCE):
            columns = range(first, first + AT_ONCE)
            loaded = [
                narrow[pl.ds(view * BZ * LINE + c, BZ, stride=LINE), :] for c in columns
            ]
            rows = pl.ds(pl.multiple_of(view * EZ, EZ), EZ)
            product = dot(
                matrix[rows, : 3 * BZ], jnp.concatenate([terms(v) for v in loaded], axis=1)
            )
            for i, column in enumerate(columns):
                wide[pl.ds(view * BX + column, EZ, stride=PITCH), :] = product[
                    :, i * NY : (i + 1) * NY
                ]
        return carry

    lax.fori_loop(0, VIEWS, one, 0, unroll=True)


def along_x_back(matrix, wide, pieces, starts):
    parts = [matrix[pl.ds(i * EX, EX), :VU] for i in range(3)]
    matrix = jnp.concatenate(parts, axis=1)
    for piece, start in zip(pieces, starts):
        for first in range(0, BZ, AT_ONCE):
            planes = range(first, first + AT_ONCE)
            loaded = [
                wide[pl.ds(pl.multiple_of((start + p) * PITCH, 8), VU), :] for p in planes
            ]
            product = dot(matrix, jnp.concatenate([terms(v) for v in loaded], axis=1))
            for i, plane in enumerate(planes):
                piece[plane] = product[:, i * NY : (i + 1) * NY]


def back_steps(core, where, back, got, blur, own, inside, outside, wide, narrow):
    z_back, x_back, y_back = views_of(back)
    for view in range(VIEWS):
        data = [got[pl.ds(where[view * BZ + plane], BX), :] for plane in range(BZ)]
        ratio = jnp.concatenate(data, axis=0) / blur[rows_of(view), :]
        value = along_y(y_back[pl.ds(view * 3 * NY, 3 * NY), :], ratio)
        for plane, rows in enumerate(planes_of(view)):
            narrow[rows, :] = value[plane * BX : (plane + 1) * BX]
    along_z_back(z_back, narrow, wide)
    along_x_back(x_back, wide, [own, inside, outside], placed(core[0]))


def first_back_kernel(
    core, back, got, blur, where, own, inside, outside,
    wide, narrow, names, slots, sem,
):
    named = got[pl.ds(SEND * BX, PEERS, stride=CHUNK), :].astype(jnp.int32)
    names[...] = jnp.transpose(jnp.concatenate([named, named], axis=0))[:8]
    copy = pltpu.make_async_copy(names, slots, sem)
    copy.start()
    copy.wait()
    for peer in range(PEERS):
        for rank in range(SEND):
            where[slots[rank, peer]] = peer * CHUNK + rank * BX
    back_steps(core, where, back, got, blur, own, inside, outside, wide, narrow)


def first_back(core, back, got, blur):
    return pl.pallas_call(
        first_back_kernel,
        out_shape=[shape((NY,), jnp.int32)] + [shape((BZ, EX, NY))] * 3,
        in_specs=[SMEM] + [VMEM] * 3,
        out_specs=[SMEM] + [VMEM] * 3,
        scratch_shapes=[
            pltpu.VMEM((EZ * PITCH, NY), F32),
            pltpu.VMEM((SLOTS * LINE, NY), F32),
            pltpu.VMEM((8, NY), jnp.int32),
            pltpu.SMEM((8, NY), jnp.int32),
            pltpu.SemaphoreType.DMA,
        ],
        compiler_params=params(24),
        name="first_back",
    )(core, back, got, blur)


def later_kernel(
    core, background, where, z_fwd, x_fwd, y_fwd, back,
    e_own, e_inside, e_outside, got, own, inside, outside, wide, narrow, blur,
):
    forward_kernel(
        core, background, z_fwd, x_fwd, y_fwd, e_own, e_inside, e_outside, blur, wide, narrow
    )
    back_steps(core, where, back, got, blur, own, inside, outside, wide, narrow)


def later(core, background, where, forth, back, pieces, got):
    return pl.pallas_call(
        later_kernel,
        out_shape=[shape((BZ, EX, NY))] * 3,
        in_specs=[SMEM] * 3 + [VMEM] * 8,
        out_specs=[VMEM] * 3,
        scratch_shapes=[
            pltpu.VMEM((EZ * PITCH, NY), F32),
            pltpu.VMEM((SLOTS * LINE, NY), F32),
            pltpu.VMEM((SLOTS * BX, NY), F32),
        ],
        compiler_params=params(24),
        name="forward_and_back",
    )(core, background, where, *forth, back, *pieces, got)


def swaps(first, count):
    pairs = [(i, i + 1) for i in range(first, count - 1, 2)]
    return pairs + [(j, i) for i, j in pairs]


def to_partners(to_even, to_odd):
    return lax.ppermute(to_even, "xy", swaps(0, PEERS)), lax.ppermute(to_odd, "xy", swaps(1, PEERS))


def past_partners(past_even, past_odd):
    right = [(i, i + 2) for i in range(PEERS - 2)]
    one = [p for p in right if p[0] % 2 == 0] + [(j, i) for i, j in right if i % 2 == 1]
    two = [(j, i) for i, j in one]
    return lax.ppermute(past_even, "xy", one), lax.ppermute(past_odd, "xy", two)


def above_and_below(block):
    count = lax.axis_size("gz")
    return lax.ppermute(block, "gz", swaps(0, count)), lax.ppermute(block, "gz", swaps(1, count))


def slab_sum(own, inside, outside):
    count = lax.axis_size("gz")
    return (
        own
        + lax.ppermute(outside, "gz", swaps(1, count))
        + lax.ppermute(inside, "gz", swaps(0, count))
    )


def three_sums(total):
    even, odd = to_partners(total[:, : 2 * BX], total[:, BX:])
    behind_odd, behind_even = past_partners(total[:, :BX], total[:, 2 * BX :])
    return jnp.concatenate(
        [
            total[:, :BX] + even[:, BX:] + behind_even,
            total[:, BX : 2 * BX] + even[:, :BX] + odd[:, BX:],
            total[:, 2 * BX :] + odd[:, :BX] + behind_odd,
        ],
        axis=1,
    )


def own_sum(total):
    even, odd = to_partners(total[:, :BX], total[:, 2 * BX :])
    return total[:, BX : 2 * BX] + even + odd


def local(
    tile_planes,
    plane_owner,
    plane_slot,
    view_shift,
    psf_z,
    psf_x,
    psf_y,
    background,
    initial_estimate,
):
    core = lax.rem(lax.axis_index("gz"), 2).astype(jnp.int32).reshape(1)
    index = lax.axis_index("xy").astype(jnp.int32).reshape(1)
    named = plane_owner.reshape(1, SRC) * NY + plane_slot.reshape(1, SRC)
    send = pack(jnp.pad(named, ((0, 0), (0, NY - SRC))), tile_planes[0])
    even, odd = to_partners(initial_estimate, initial_estimate)
    send, even, odd = lax.optimization_barrier((send, even, odd))
    got = lax.all_to_all(
        send.reshape(PEERS, 1, CHUNK * NY), "xy", split_axis=0, concat_axis=0, tiled=True
    ).reshape(PEERS * CHUNK, NY)
    psf = jnp.concatenate([psf_z, psf_x, psf_y], axis=0)
    taps = psf / jnp.sum(psf, axis=1, keepdims=True)
    *forth, back = weights(index, taps, view_shift)
    bricks = jnp.concatenate([even, initial_estimate, odd], axis=1)
    for step in range(ITERS):
        pieces = (bricks, *above_and_below(bricks))
        if step == 0:
            blur = forward(core, background, *forth, *pieces)
            where, *parts = first_back(core, back, got, blur)
        else:
            parts = later(core, background, where, forth, back, pieces, got)
        total = slab_sum(*parts)
        if step + 1 < ITERS:
            bricks = bricks * (three_sums(total) / VIEWS)
    return bricks[:, BX : 2 * BX] * (own_sum(total) / VIEWS)


def solution(mesh):
    return jax.shard_map(
        local,
        mesh=mesh,
        in_specs=(
            P("gz", "xy", None),
            P("gz", "xy", None),
            P("gz", "xy"),
            P(),
            P(),
            P(),
            P(),
            P(),
            P("gz", "xy", None),
        ),
        out_specs=P("gz", "xy", None),
        check_vma=False,
    )
```

```python
import jax
import jax.numpy as jnp
from jax import lax
from jax.experimental import pallas as pl
from jax.experimental.pallas import tpu as pltpu
from jax.sharding import PartitionSpec as P

ITERS = 2
VIEWS = 6
TAPS = 33
R = 16
BZ = 16
BX = 16
NY = 128
SEND = 3
SRC = 96
PEERS = 64
EX = BX + 2 * R
EZ = BZ + 2 * R
SLOTS = VIEWS * BZ
CHUNK = SEND * BX + 1
VU = VIEWS * BX
PITCH = VU + 8
LINE = BX + 8
AT_ONCE = 4
F32 = jnp.float32
BF16 = jnp.bfloat16

VMEM = pl.BlockSpec(memory_space=pltpu.VMEM)
SMEM = pl.BlockSpec(memory_space=pltpu.SMEM)


def params(mib):
    return pltpu.CompilerParams(vmem_limit_bytes=mib * 1024 * 1024)


def shape(dims, dtype=F32):
    return jax.ShapeDtypeStruct(dims, dtype)


def split(value):
    high = value.astype(BF16)
    return high, (value - high.astype(F32)).astype(BF16)


def pack_kernel(named_in, planes, send, rows, count, named, sem):
    copy = pltpu.make_async_copy(named_in, named, sem)
    copy.start()
    for peer in range(PEERS):
        count[peer] = 0
    send[pl.ds(SEND * BX, PEERS, stride=CHUNK), :] = jnp.full((PEERS, NY), SLOTS, F32)
    for group in range(SRC // 8):
        for column in range(BX):
            rows[pl.ds(group * 8 * LINE + column, 8, stride=LINE), :] = planes[
                group * 8 : group * 8 + 8, column * NY : (column + 1) * NY
            ]
    lane = lax.broadcasted_iota(jnp.int32, (1, NY), 1)
    copy.wait()

    def place(plane, carry):
        peer = named[0, plane] >> 7
        rank = count[peer]
        count[peer] = rank + 1
        start = peer * CHUNK
        send[pl.ds(start + rank * BX, BX), :] = rows[pl.ds(pl.multiple_of(plane * LINE, 8), BX), :]
        pltpu.store(
            send.at[pl.ds(start + SEND * BX, 1), :],
            jnp.full((1, NY), named[0, plane] & (NY - 1), jnp.int32).astype(F32),
            mask=lane == rank,
        )
        return carry

    lax.fori_loop(0, SRC, place, 0, unroll=8)


def pack(named, planes):
    return pl.pallas_call(
        pack_kernel,
        out_shape=shape((PEERS * CHUNK, NY)),
        in_specs=[VMEM, VMEM],
        out_specs=VMEM,
        scratch_shapes=[
            pltpu.VMEM((SRC * LINE, NY), F32),
            pltpu.SMEM((PEERS,), jnp.int32),
            pltpu.SMEM((1, NY), jnp.int32),
            pltpu.SemaphoreType.DMA,
        ],
        compiler_params=params(16),
        name="pack_planes",
    )(named, planes)


def bands(taps, first, place):
    row = lax.broadcasted_iota(jnp.int32, (BX, NY), 0)
    lane = place(lax.broadcasted_iota(jnp.int32, (BX, NY), 1))
    each = []
    for view in range(VIEWS):
        band = jnp.zeros((BX, NY), F32)
        for tap in range(TAPS):
            band = jnp.where(lane - row == tap, taps[first + view, tap], band)
        each.append(band)
    return jnp.concatenate(each + [jnp.zeros((NY - VU, NY), F32)], axis=0)


def by_terms(value):
    high, low = split(value)
    return jnp.concatenate([high, low, high], axis=1)


def views_of(ref):
    z_rows, x_rows = VIEWS * EZ, 2 * EX
    return (
        ref.at[pl.ds(0, z_rows), :],
        ref.at[pl.ds(z_rows, x_rows), :],
        ref.at[pl.ds(z_rows + x_rows, VIEWS * 3 * NY), :],
    )


def weight_kernel(index, taps, shift, z_fwd, x_fwd, y_fwd, back):
    z_back, x_back, y_back = views_of(back)
    band = bands(taps, 0, lambda lane: lane)
    turned = jnp.transpose(band)[:EZ]
    for view in range(VIEWS):
        z_fwd[view] = by_rows(band[view * BZ : (view + 1) * BZ, :EZ])
        z_back[pl.ds(view * EZ, EZ), : 3 * BZ] = by_terms(turned[:, view * BZ : (view + 1) * BZ])
    flip = jnp.where(index[0] % 2 == 0, 2 * BX, 0)
    band = bands(
        taps,
        VIEWS,
        lambda lane: jnp.where(
            lane < BX, lane + flip, jnp.where((lane >= 2 * BX) & (lane < EX), lane - flip, lane)
        ),
    )
    x_fwd[...] = by_terms(band[:VU, :EX])
    high, low = split(jnp.transpose(band)[:EX, :VU])
    for i, part in enumerate([high, low]):
        x_back[pl.ds(i * EX, EX), :VU] = part
    row = lax.broadcasted_iota(jnp.int32, (NY, NY), 0)
    lane = lax.broadcasted_iota(jnp.int32, (NY, NY), 1)

    def along_y(view, carry):
        offset = lane - row + R + shift[view]
        back = jnp.zeros((NY, NY), F32)
        for tap in range(TAPS):
            back = jnp.where(offset == tap, taps[2 * VIEWS + view, tap], back)
        high, low = split(back)
        y_back[pl.ds(pl.multiple_of(view * 3 * NY, NY), 3 * NY), :] = jnp.concatenate(
            [high, low, high], axis=0
        )
        high, low = split(jnp.transpose(back))
        y_fwd[view] = jnp.concatenate([high, low, high], axis=0)
        return carry

    lax.fori_loop(0, VIEWS, along_y, 0)


def weights(index, taps, shift):
    return pl.pallas_call(
        weight_kernel,
        out_shape=[
            shape((VIEWS, 2 * BZ, 2 * EZ), BF16),
            shape((VU, 3 * EX), BF16),
            shape((VIEWS, 3 * NY, NY), BF16),
            shape((VIEWS * EZ + 2 * EX + VIEWS * 3 * NY, NY), BF16),
        ],
        in_specs=[SMEM] * 3,
        out_specs=[VMEM] * 4,
        compiler_params=params(16),
        name="operator_matrices",
    )(index, taps, shift)


def dot(left, right):
    return jnp.dot(left, right, preferred_element_type=F32)


def by_rows(value):
    high, low = split(value)
    upper = jnp.concatenate([high, high], axis=1)
    return jnp.concatenate([upper, jnp.concatenate([low, jnp.zeros_like(low)], axis=1)], axis=0)


def dot_by_rows(matrix, values):
    pairs = [jnp.concatenate(split(value), axis=0) for value in values]
    product = dot(matrix, jnp.concatenate(pairs, axis=1))
    half = product.shape[0] // 2
    return product[:half] + product[half:]


def terms(value):
    high, low = split(value)
    return jnp.concatenate([high, high, low], axis=0)


def along_x_fwd(matrix, pieces, starts, wide):
    matrix = matrix[...]
    for piece, start in zip(pieces, starts):
        for first in range(0, BZ, AT_ONCE):
            planes = range(first, first + AT_ONCE)
            product = dot(matrix, jnp.concatenate([terms(piece[p]) for p in planes], axis=1))
            for i, plane in enumerate(planes):
                rows = pl.ds(pl.multiple_of((start + plane) * PITCH, 8), VU)
                wide[rows, :] = product[:, i * NY : (i + 1) * NY]


def along_z_fwd(matrix, wide, narrow):
    def one(view, carry):
        for first in range(0, BX, AT_ONCE):
            columns = range(first, first + AT_ONCE)
            loaded = [wide[pl.ds(view * BX + c, EZ, stride=PITCH), :] for c in columns]
            product = dot_by_rows(matrix[view], loaded)
            for i, column in enumerate(columns):
                rows = pl.ds(view * BZ * LINE + column, BZ, stride=LINE)
                narrow[rows, :] = product[:, i * NY : (i + 1) * NY]
        return carry

    lax.fori_loop(0, VIEWS, one, 0, unroll=True)


def rows_of(view):
    return pl.ds(view * BZ * BX, BZ * BX)


def planes_of(view):
    starts = [(view * BZ + plane) * LINE for plane in range(BZ)]
    return [pl.ds(start, BX) for start in starts]


def along_y(matrix, value):
    high, low = split(value)
    return dot(jnp.concatenate([high, high, low], axis=1), matrix)


def placed():
    core = lax.rem(lax.axis_index("gz"), 2)
    inside = jnp.where(core == 0, 2 * R, 0)
    outside = jnp.where(core == 0, 0, 2 * R)
    return [R, inside, outside]


def forward_kernel(
    background, z_fwd, x_fwd, y_fwd, own, inside, outside, blur, wide, narrow
):
    along_x_fwd(x_fwd, [own, inside, outside], placed(), wide)
    along_z_fwd(z_fwd, wide, narrow)
    for view in range(VIEWS):
        value = jnp.concatenate([narrow[rows, :] for rows in planes_of(view)], axis=0)
        blur[rows_of(view), :] = along_y(y_fwd[view], value) + background[view : view + 1, :]


def forward(background, z_fwd, x_fwd, y_fwd, own, inside, outside):
    return pl.pallas_call(
        forward_kernel,
        out_shape=shape((SLOTS * BX, NY)),
        in_specs=[VMEM] * 7,
        out_specs=VMEM,
        scratch_shapes=[pltpu.VMEM((EZ * PITCH, NY), F32), pltpu.VMEM((SLOTS * LINE, NY), F32)],
        compiler_params=params(24),
        name="forward",
    )(background, z_fwd, x_fwd, y_fwd, own, inside, outside)


def along_z_back(matrix, narrow, wide):
    def one(view, carry):
        for first in range(0, BX, AT_ONCE):
            columns = range(first, first + AT_ONCE)
            loaded = [
                narrow[pl.ds(view * BZ * LINE + c, BZ, stride=LINE), :] for c in columns
            ]
            rows = pl.ds(pl.multiple_of(view * EZ, EZ), EZ)
            product = dot(
                matrix[rows, : 3 * BZ], jnp.concatenate([terms(v) for v in loaded], axis=1)
            )
            for i, column in enumerate(columns):
                wide[pl.ds(view * BX + column, EZ, stride=PITCH), :] = product[
                    :, i * NY : (i + 1) * NY
                ]
        return carry

    lax.fori_loop(0, VIEWS, one, 0, unroll=True)


def along_x_back(matrix, wide, pieces, starts):
    high, low = [matrix[pl.ds(i * EX, EX), :VU] for i in range(2)]
    upper = jnp.concatenate([high, high], axis=1)
    lower = jnp.concatenate([low, jnp.zeros_like(low)], axis=1)
    matrix = jnp.concatenate([upper, lower], axis=0)
    for piece, start in zip(pieces, starts):
        for first in range(0, BZ, AT_ONCE):
            planes = range(first, first + AT_ONCE)
            loaded = [
                wide[pl.ds(pl.multiple_of((start + p) * PITCH, 8), VU), :] for p in planes
            ]
            product = dot_by_rows(matrix, loaded)
            for i, plane in enumerate(planes):
                piece[plane] = product[:, i * NY : (i + 1) * NY]


def back_steps(where, back, got, blur, own, inside, outside, wide, narrow):
    z_back, x_back, y_back = views_of(back)
    for view in range(VIEWS):
        data = [got[pl.ds(where[view * BZ + plane], BX), :] for plane in range(BZ)]
        ratio = jnp.concatenate(data, axis=0) / blur[rows_of(view), :]
        value = along_y(y_back[pl.ds(view * 3 * NY, 3 * NY), :], ratio)
        for plane, rows in enumerate(planes_of(view)):
            narrow[rows, :] = value[plane * BX : (plane + 1) * BX]
    along_z_back(z_back, narrow, wide)
    along_x_back(x_back, wide, [own, inside, outside], placed())


def slot_copy(got, names, slots, sem):
    named = got[pl.ds(SEND * BX, PEERS, stride=CHUNK), :].astype(jnp.int32)
    names[...] = jnp.transpose(jnp.concatenate([named, named], axis=0))[:8]
    return pltpu.make_async_copy(names, slots, sem)


def fill_table(slots, where):
    for peer in range(PEERS):
        for rank in range(SEND):
            where[slots[rank, peer]] = peer * CHUNK + rank * BX


SCRATCH = [
    pltpu.VMEM((EZ * PITCH, NY), F32),
    pltpu.VMEM((SLOTS * LINE, NY), F32),
    pltpu.VMEM((8, NY), jnp.int32),
    pltpu.SMEM((8, NY), jnp.int32),
    pltpu.SMEM((NY,), jnp.int32),
    pltpu.SemaphoreType.DMA,
]


def first_back_kernel(
    back, got, blur, own, inside, outside, wide, narrow, names, slots, where, sem
):
    copy = slot_copy(got, names, slots, sem)
    copy.start()
    copy.wait()
    fill_table(slots, where)
    back_steps(where, back, got, blur, own, inside, outside, wide, narrow)


def first_back(back, got, blur):
    return pl.pallas_call(
        first_back_kernel,
        out_shape=[shape((BZ, EX, NY))] * 3,
        in_specs=[VMEM] * 3,
        out_specs=[VMEM] * 3,
        scratch_shapes=SCRATCH,
        compiler_params=params(24),
        name="first_back",
    )(back, got, blur)


def later_kernel(
    background, z_fwd, x_fwd, y_fwd, back, e_own, e_inside, e_outside, got, own, inside, outside,
    wide, narrow, names, slots, where, sem, blur,
):
    copy = slot_copy(got, names, slots, sem)
    copy.start()
    forward_kernel(
        background, z_fwd, x_fwd, y_fwd, e_own, e_inside, e_outside, blur, wide, narrow
    )
    copy.wait()
    fill_table(slots, where)
    back_steps(where, back, got, blur, own, inside, outside, wide, narrow)


def later(background, forth, back, pieces, got):
    return pl.pallas_call(
        later_kernel,
        out_shape=[shape((BZ, EX, NY))] * 3,
        in_specs=[VMEM] * 9,
        out_specs=[VMEM] * 3,
        scratch_shapes=SCRATCH + [pltpu.VMEM((SLOTS * BX, NY), F32)],
        compiler_params=params(24),
        name="forward_and_back",
    )(background, *forth, back, *pieces, got)


def swaps(first, count):
    pairs = [(i, i + 1) for i in range(first, count - 1, 2)]
    return pairs + [(j, i) for i, j in pairs]


def to_partners(to_even, to_odd):
    return lax.ppermute(to_even, "xy", swaps(0, PEERS)), lax.ppermute(to_odd, "xy", swaps(1, PEERS))


def past_partners(past_even, past_odd):
    right = [(i, i + 2) for i in range(PEERS - 2)]
    one = [p for p in right if p[0] % 2 == 0] + [(j, i) for i, j in right if i % 2 == 1]
    two = [(j, i) for i, j in one]
    return lax.ppermute(past_even, "xy", one), lax.ppermute(past_odd, "xy", two)


def above_and_below(block):
    count = lax.axis_size("gz")
    return lax.ppermute(block, "gz", swaps(0, count)), lax.ppermute(block, "gz", swaps(1, count))


def slab_sum(own, inside, outside):
    count = lax.axis_size("gz")
    return (
        own
        + lax.ppermute(outside, "gz", swaps(1, count))
        + lax.ppermute(inside, "gz", swaps(0, count))
    )


def three_sums(total):
    even, odd = to_partners(total[:, : 2 * BX], total[:, BX:])
    behind_odd, behind_even = past_partners(total[:, :BX], total[:, 2 * BX :])
    return jnp.concatenate(
        [
            total[:, :BX] + even[:, BX:] + behind_even,
            total[:, BX : 2 * BX] + even[:, :BX] + odd[:, BX:],
            total[:, 2 * BX :] + odd[:, :BX] + behind_odd,
        ],
        axis=1,
    )


def own_sum(total):
    even, odd = to_partners(total[:, :BX], total[:, 2 * BX :])
    return total[:, BX : 2 * BX] + even + odd


def local(
    tile_planes,
    plane_owner,
    plane_slot,
    view_shift,
    psf_z,
    psf_x,
    psf_y,
    background,
    initial_estimate,
):
    index = lax.axis_index("xy").astype(jnp.int32).reshape(1)
    named = plane_owner.reshape(1, SRC) * NY + plane_slot.reshape(1, SRC)
    send = pack(jnp.pad(named, ((0, 0), (0, NY - SRC))), tile_planes[0])
    even, odd = to_partners(initial_estimate, initial_estimate)
    send, even, odd = lax.optimization_barrier((send, even, odd))
    got = lax.all_to_all(
        send.reshape(PEERS, 1, CHUNK * NY), "xy", split_axis=0, concat_axis=0, tiled=True
    ).reshape(PEERS * CHUNK, NY)
    psf = jnp.concatenate([psf_z, psf_x, psf_y], axis=0)
    taps = psf / jnp.sum(psf, axis=1, keepdims=True)
    *forth, back = weights(index, taps, view_shift)
    levels = jnp.broadcast_to(background[:, None], (VIEWS, NY))
    bricks = jnp.concatenate([even, initial_estimate, odd], axis=1)
    for step in range(ITERS):
        pieces = (bricks, *above_and_below(bricks))
        if step == 0:
            blur = forward(levels, *forth, *pieces)
            parts = first_back(back, got, blur)
        else:
            parts = later(levels, forth, back, pieces, got)
        total = slab_sum(*parts)
        if step + 1 < ITERS:
            bricks = bricks * (three_sums(total) / VIEWS)
    return bricks[:, BX : 2 * BX] * (own_sum(total) / VIEWS)


def solution(mesh):
    return jax.shard_map(
        local,
        mesh=mesh,
        in_specs=(
            P("gz", "xy", None),
            P("gz", "xy", None),
            P("gz", "xy"),
            P(),
            P(),
            P(),
            P(),
            P(),
            P("gz", "xy", None),
        ),
        out_specs=P("gz", "xy", None),
        check_vma=False,
    )
```
